256 devices in a mesh: dp: 8 (over y, x_hi), expert: 16 (over x_lo, z), tensor: 2 (over core).
Axes of the slice: x: 4 (x_hi: 2, x_lo: 2; x = x_hi * 2 + x_lo), y: 4, z: 8, core: 2. Of those that a mesh axis runs over, the one named last changes fastest.
Arguments:
- tokens: bfloat16 [16384, 4096], P(('dp', 'expert'), 'tensor'), may hold values from -6 to 6
- routes: int32 [16384, 2], P(('dp', 'expert')), may hold values from 0 to 14, as said below
- gates: float32 [16384, 2], P(('dp', 'expert')), may hold values from 0.2 to 1
- dropped: int32 [16384, 2], P(('dp', 'expert')), may hold values from 0 to 1, as said below
- placement: int32 [15], replicated, may hold values from 0 to 15, as said below
- w_gate: bfloat16 [16, 4096, 768], P('expert', None, 'tensor'), may hold values from -0.09375 to 0.09375
- w_up: bfloat16 [16, 4096, 768], P('expert', None, 'tensor'), may hold values from -0.09375 to 0.09375
- w_down: bfloat16 [16, 768, 4096], P('expert', 'tensor'), may hold values from -0.21875 to 0.21875
- cotangent: bfloat16 [16384, 4096], P(('dp', 'expert'), 'tensor'), may hold values from -1.1953125 to 1.1953125
Outputs:
- mixed: bfloat16 [16384, 4096], P(('dp', 'expert'), 'tensor')
- input_grad: bfloat16 [16384, 4096], P(('dp', 'expert'), 'tensor')
- grad_gate: bfloat16 [16, 4096, 768], P('expert', 'dp', 'tensor')
- grad_up: bfloat16 [16, 4096, 768], P('expert', 'dp', 'tensor')
- grad_down: bfloat16 [16, 768, 4096], P('expert', 'tensor', 'dp')
The draws below stay inside these ranges and needn't reach their ends.
Inputs may be any that keep to these rules, and one draw needn't show every extreme that they name: `routes`: each token names 2 different experts below 15; one expert, the same in every block, is named by every token. `dropped`: within an aligned block of 128 tokens every expert keeps at most 32 routes, and the expert named by every token keeps exactly 32 in every block. `placement`: 15 distinct slots below 16; one slot, neither the first nor the last, hosts no expert.
All inputs are finite; a program needn't handle non-finite values.
Results may differ from the reference program's by a relative error of at most 0.017.
Values may be sent and summed in bfloat16 or wider, within the bound.
A program may use at most 192 MiB of HBM per device.

```python
import jax
import jax.numpy as jnp
from jax import lax

D = 4096
FFW = 768
TOK_DEV = 128
TOP = 2
SLOTS = 16
EXPERTS = 15
GROUPS = 8
TOKENS = 16384
CAP = 32


def route_draw(key):
    key_hot, key_score, key_bias, key_order, key_cut = jax.random.split(key, 5)
    hot_expert = jax.random.randint(key_hot, (), 0, EXPERTS)
    labels = jnp.arange(EXPERTS, dtype=jnp.int32)
    noise_term = jax.random.randint(key_score, (TOKENS, EXPERTS), 0, 65536)
    bias_level = jax.random.randint(key_bias, (EXPERTS,), 0, 4)
    scores = (noise_term + bias_level[None, :] * 32768) * EXPERTS + labels[None, :]
    scores = jnp.where(labels[None, :] == hot_expert, scores + (1 << 28), scores)
    unused, chosen = lax.top_k(scores, TOP)
    column_order = jax.random.randint(key_order, (TOKENS, TOP), 0, 4096) * TOP + jnp.arange(TOP, dtype=jnp.int32)[None, :]
    shuffle = jnp.argsort(column_order, axis=1, stable=True)
    chosen = jnp.take_along_axis(chosen, shuffle, axis=1).astype(jnp.int32)
    extra_cut = (jax.random.randint(key_cut, (TOKENS, TOP), 0, 8) == 0) & (chosen != hot_expert)
    block_count = TOKENS // TOK_DEV
    flat_routes = chosen.reshape(block_count, TOK_DEV * TOP)
    alive_mask = jnp.logical_not(extra_cut).reshape(block_count, TOK_DEV * TOP)
    hit_table = jnp.where((flat_routes[:, :, None] == labels[None, None, :]) & alive_mask[:, :, None], 1, 0).astype(jnp.int32)
    before = jnp.cumsum(hit_table, axis=1) - hit_table
    rank_in_block = jnp.sum(before * hit_table, axis=2)
    keep_mask = alive_mask & (rank_in_block < CAP)
    dropped = jnp.where(keep_mask, 0, 1).reshape(TOKENS, TOP).astype(jnp.int32)
    return (chosen, dropped)


def draw_routes(key, part):
    return route_draw(key)[0]


def draw_dropped(key, part):
    return route_draw(key)[1]


def draw_placement(key, part):
    key = jax.random.fold_in(key, 7)
    key_empty, key_order = jax.random.split(key, 2)
    empty_slot = jax.random.randint(key_empty, (), 1, SLOTS - 1)
    order = jax.random.permutation(key_order, EXPERTS).astype(jnp.int32)
    return jnp.where(order >= empty_slot, order + 1, order).astype(jnp.int32)


def steps_of(own_key, extent, pieces, least, high):
    def one(axis_at, blocks):
        draws = jax.random.uniform(jax.random.fold_in(jax.random.fold_in(own_key, 6), axis_at), (blocks,), jnp.float32, least / len(pieces), high / len(pieces))
        return jnp.repeat(jnp.exp(draws), extent[axis_at] // blocks).reshape((-1,) + (1,) * (len(extent) - axis_at - 1))

    loudness = one(*pieces[0])
    for cut in pieces[1:]:
        loudness = loudness * one(*cut)
    return loudness


def gaussian(key, shape, spread, limit, shards=(), held_as=jnp.bfloat16):
    loudness = steps_of(key, shape, shards, -0.22, 0.18) if shards else 1.0
    entries = jax.random.normal(key, shape, jnp.float32) * spread * loudness
    return jnp.minimum(jnp.maximum(entries, -limit), limit).astype(held_as)


def setup_inputs(seed: int = 0) -> dict:
    key_of = jax.random.split(jax.random.key(seed), 10)
    return {
        "tokens": gaussian(key_of[0], (TOKENS, D), 1.0, 6.0, ((0, 128), (1, 2))),
        "routes": draw_routes(jax.random.fold_in(key_of[9], 71), 0),
        "gates": jnp.clip(0.2 + 0.8 * jax.random.uniform(key_of[2], (TOKENS, TOP), jnp.float32) ** steps_of(key_of[2], (TOKENS, TOP), ((0, 128),), -0.2, 0.2), 0.2, 1.0),
        "dropped": draw_dropped(jax.random.fold_in(key_of[9], 71), 0),
        "placement": draw_placement(jax.random.fold_in(key_of[9], 71), 0),
        "w_gate": gaussian(key_of[5], (SLOTS, D, FFW), D ** -0.5, 0.09375, ((0, 16), (2, 2))),
        "w_up": gaussian(key_of[6], (SLOTS, D, FFW), D ** -0.5, 0.09375, ((0, 16), (2, 2))),
        "w_down": gaussian(key_of[7], (SLOTS, FFW, D), FFW ** -0.5, 0.21875, ((0, 16), (1, 2))),
        "cotangent": gaussian(key_of[8], (TOKENS, D), 0.2, 1.1953125, ((0, 128), (1, 2))),
    }


def buffer_rows(routes, dropped, placement):
    block_count = TOKENS // TOK_DEV
    block_routes = TOK_DEV * TOP
    flat_routes = routes.reshape(block_count, block_routes)
    kept_mask = dropped.reshape(block_count, block_routes) == 0
    labels = jnp.arange(EXPERTS, dtype=jnp.int32)
    hit_table = jnp.where((flat_routes[:, :, None] == labels[None, None, :]) & kept_mask[:, :, None], 1, 0).astype(jnp.int32)
    before = jnp.cumsum(hit_table, axis=1) - hit_table
    position = jnp.sum(before * hit_table, axis=2)
    target = jnp.sum(hit_table * placement[None, None, :], axis=2)
    return jnp.where(kept_mask, target * CAP + position, -1).astype(jnp.int32), kept_mask


def reference(tokens, routes, gates, dropped, placement, w_gate, w_up, w_down, cotangent):
    block_count = TOKENS // TOK_DEV
    block_routes = TOK_DEV * TOP
    row_of, kept_mask = buffer_rows(routes, dropped, placement)
    route_gate = jnp.where(kept_mask, gates.reshape(block_count, block_routes), 0.0).astype(jnp.float32)
    token_blocks = tokens.reshape(block_count, TOK_DEV, D)
    grad_blocks = cotangent.reshape(block_count, TOK_DEV, D)
    route_ids = jnp.arange(block_routes, dtype=jnp.int32)
    block_index = jnp.arange(block_count, dtype=jnp.int32)[:, None]
    contract = (((1,), (1,)), ((), ()))

    def slot_step(totals, slot_index):
        mixed_sum, input_sum = totals
        row_ids = slot_index * CAP + jnp.arange(CAP, dtype=jnp.int32)
        matched = row_of[:, None, :] == row_ids[None, :, None]
        filled = jnp.any(matched, axis=2)
        source_route = jnp.sum(jnp.where(matched, route_ids[None, None, :], 0), axis=2).astype(jnp.int32)
        token_of = (source_route // TOP).astype(jnp.int32)
        gate_of = jnp.where(filled, route_gate[block_index, source_route], 0.0)
        expert_in = jnp.where(filled[:, :, None], token_blocks[block_index, token_of], 0.0).astype(jnp.bfloat16).reshape(-1, D)
        grad_in = (gate_of[:, :, None] * grad_blocks[block_index, token_of].astype(jnp.float32)).astype(jnp.bfloat16).reshape(-1, D)
        gate_matrix = w_gate[slot_index]
        up_matrix = w_up[slot_index]
        down_matrix = w_down[slot_index]
        gate_pre = jnp.dot(expert_in, gate_matrix, preferred_element_type=jnp.float32)
        up_pre = jnp.dot(expert_in, up_matrix, preferred_element_type=jnp.float32)
        sigmoid_gate = jax.nn.sigmoid(gate_pre)
        silu_gate = gate_pre * sigmoid_gate
        hidden = (silu_gate * up_pre).astype(jnp.bfloat16)
        expert_out = jnp.dot(hidden, down_matrix, preferred_element_type=jnp.float32).astype(jnp.bfloat16)
        grad_hidden = lax.dot_general(grad_in, down_matrix, contract, preferred_element_type=jnp.float32)
        slope = sigmoid_gate * (1.0 + gate_pre * (1.0 - sigmoid_gate))
        grad_gate_pre = (grad_hidden * up_pre * slope).astype(jnp.bfloat16)
        grad_up_pre = (grad_hidden * silu_gate).astype(jnp.bfloat16)
        both_grads = jnp.concatenate([grad_gate_pre, grad_up_pre], axis=1)
        both_weights = jnp.concatenate([gate_matrix, up_matrix], axis=1)
        grad_rows = lax.dot_general(both_grads, both_weights, contract, preferred_element_type=jnp.float32).astype(jnp.bfloat16)
        out_blocks = expert_out.reshape(block_count, CAP, D).astype(jnp.float32)
        back_blocks = grad_rows.reshape(block_count, CAP, D).astype(jnp.float32)
        mixed_sum = mixed_sum.at[block_index, token_of].add(gate_of[:, :, None] * out_blocks)
        filled_weight = jnp.where(filled, 1.0, 0.0).astype(jnp.float32)
        input_sum = input_sum.at[block_index, token_of].add(filled_weight[:, :, None] * back_blocks)
        group_in = expert_in.reshape(GROUPS, -1, D).astype(jnp.float32)
        group_grad = grad_in.reshape(GROUPS, -1, D).astype(jnp.float32)
        group_gate = grad_gate_pre.reshape(GROUPS, -1, FFW).astype(jnp.float32)
        group_up = grad_up_pre.reshape(GROUPS, -1, FFW).astype(jnp.float32)
        group_hidden = hidden.reshape(GROUPS, -1, FFW).astype(jnp.float32)
        grad_gate = jnp.sum(jnp.einsum("grd,grf->gdf", group_in, group_gate).astype(jnp.bfloat16), axis=0, dtype=jnp.float32).astype(jnp.bfloat16)
        grad_up = jnp.sum(jnp.einsum("grd,grf->gdf", group_in, group_up).astype(jnp.bfloat16), axis=0, dtype=jnp.float32).astype(jnp.bfloat16)
        grad_down = jnp.sum(jnp.einsum("grf,grd->gfd", group_hidden, group_grad).astype(jnp.bfloat16), axis=0, dtype=jnp.float32).astype(jnp.bfloat16)
        return (mixed_sum, input_sum), (grad_gate, grad_up, grad_down)

    start = (jnp.zeros((block_count, TOK_DEV, D), jnp.float32), jnp.zeros((block_count, TOK_DEV, D), jnp.float32))
    totals, stacked = lax.scan(slot_step, start, jnp.arange(SLOTS, dtype=jnp.int32))
    mixed = totals[0].reshape(TOKENS, D).astype(jnp.bfloat16)
    input_grad = totals[1].reshape(TOKENS, D).astype(jnp.bfloat16)
    return (mixed, input_grad, stacked[0], stacked[1], stacked[2])
```

```python
import jax
import jax.numpy as jnp
from jax import lax
from jax.experimental import pallas as pl
from jax.experimental.pallas import tpu as pltpu
from jax.sharding import PartitionSpec as P

MESH = pl.DeviceIdType.MESH
BF = jnp.bfloat16
F32 = jnp.float32
TOK = 128
CAP = 32
ROWS = 16 * CAP
FULL = 4096
HALF = 2048
FF = 384
COL = 512
MIB = 1 << 20

STEPS = ((0, 0), (1, 1), (1, -1), (2, 1), (2, -1))
FAR = {(1, 0): 10, (1, 1): 11, (-1, 0): 12, (-1, 1): 13, (1, 2): 14, (-1, 2): 15}


class Place:
    def __init__(self):
        self.dp = lax.axis_index("dp")
        expert = lax.axis_index("expert")
        self.core = lax.axis_index("tensor")
        self.y = lax.div(self.dp, 2)
        self.xh = lax.rem(self.dp, 2)
        self.x = lax.div(expert, 8)
        self.z = lax.rem(expert, 8)

    def slot(self, dx, dz):
        return lax.rem(self.x + dx, 2) * 8 + lax.rem(self.z + dz + 8, 8)

    def near(self, dx, dz):
        return (self.dp, self.slot(dx, dz), self.core)

    def other_core(self):
        return (self.dp, self.slot(0, 0), 1 - self.core)

    def along_y(self, dy):
        return (lax.rem(self.y + dy + 4, 4) * 2 + self.xh, self.slot(0, 0), self.core)

    def other_xh(self):
        return (self.y * 2 + 1 - self.xh, self.slot(0, 0), self.core)


def barrier(peers):
    sem = pltpu.get_barrier_semaphore()
    for peer in peers:
        pl.semaphore_signal(sem, inc=1, device_id=peer, device_id_type=MESH)
    pl.semaphore_wait(sem, len(peers))


def tree_peers(here):
    return [
        here.near(0, 1), here.near(0, -1), here.near(0, 2), here.near(0, -2), here.near(1, 0),
        here.near(1, 1), here.near(1, -1), here.near(1, 2), here.near(1, -2), here.other_core(),
    ]


def remote(src, dst, send, recv, peer):
    return pltpu.make_async_remote_copy(
        src_ref=src, dst_ref=dst, send_sem=send, recv_sem=recv, device_id=peer, device_id_type=MESH
    )


def slots_of(here, index):
    slots = [here.slot(0, 0), here.slot(1, 0)]
    depth, way = STEPS[index]
    if depth == 2:
        slots += [here.slot(0, way), here.slot(1, way)]
        slots.append(here.slot(0, 2) if way == 1 else here.slot(1, -2))
    return slots


def far_places(index):
    way = STEPS[index][1]
    return [FAR[(way, n)] for n in range(3)]


def far_peer(here, way, n, sign):
    if n == 0:
        return here.near(0, way * sign)
    if n == 1:
        return here.near(1, way * sign)
    return here.near(0, 2 * sign) if way == 1 else here.near(1, -2 * sign)


def hits(meta, slots):
    ids = jnp.concatenate(
        [(s * CAP + lax.broadcasted_iota(jnp.int32, (CAP, TOK), 0)).astype(F32) for s in slots], axis=0
    )
    return meta[0:1, :] == ids, meta[1:2, :] == ids


def plain_table(meta, slots):
    first, second = hits(meta, slots)
    return jnp.where(first | second, 1.0, 0.0).astype(F32)


def gate_table(meta, slots):
    first, second = hits(meta, slots)
    return jnp.where(first, meta[2:3, :], 0.0) + jnp.where(second, meta[3:4, :], 0.0)


def make_meta(routes, gates, place):
    label = lax.broadcasted_iota(jnp.int32, (16, TOK), 0)
    kept = [routes[2 + k : 3 + k, :] == 0 for k in range(2)]
    hit = [jnp.where((routes[k : k + 1, :] == label) & kept[k], 1.0, 0.0).astype(F32) for k in range(2)]
    earlier = lax.broadcasted_iota(jnp.int32, (TOK, TOK), 0) < lax.broadcasted_iota(jnp.int32, (TOK, TOK), 1)
    before = jnp.dot(
        (hit[0] + hit[1]).astype(BF), jnp.where(earlier, 1.0, 0.0).astype(BF), preferred_element_type=F32
    )
    base = place.astype(F32) * CAP
    row = [
        jnp.sum(hit[0] * (before + base), axis=0, keepdims=True),
        jnp.sum(hit[1] * (before + hit[0] + base), axis=0, keepdims=True),
    ]
    out = [jnp.where(kept[k], row[k], -1.0) for k in range(2)]
    out += [jnp.where(kept[k], gates[k : k + 1, :], 0.0) for k in range(2)]
    out.append(jnp.zeros((4, TOK), F32))
    return jnp.concatenate(out, axis=0)


def dispatch_kernel(
    routes, gates, place, tok, cot, rows_tok, rows_cot, metas,
    comp, sendb, meta_send, meta_recv, hop_send, hop_recv, far_send, far_recv, core_send, core_recv,
):
    here = Place()
    metas[0] = make_meta(routes[...], gates[...], place[...])
    barrier(tree_peers(here))
    started = []

    def start(copy):
        copy.start()
        started.append(copy)
        return copy

    for i in range(1, 5):
        depth, way = STEPS[i]
        start(remote(metas.at[0], metas.at[i], meta_send.at[i - 1], meta_recv.at[i - 1], here.near(0, way * depth)))
    source = (tok, cot)
    final = (rows_tok, rows_cot)
    mine = pl.ds(pl.multiple_of(here.core * HALF, HALF), HALF)
    hop = {}

    def first_hop(a):
        for i in (1, 2):
            hop[a, i] = start(
                remote(source[a], comp.at[a, i - 1], hop_send.at[a, i - 1], hop_recv.at[a, i - 1], here.near(0, STEPS[i][1]))
            )

    def second_hop(a, i):
        hop[a, i].wait_recv()
        hop[a, i + 2] = start(
            remote(comp.at[a, i - 1], comp.at[a, i + 1], hop_send.at[a, i + 1], hop_recv.at[a, i + 1], here.near(0, STEPS[i][1]))
        )

    core = {}

    def to_core(a, j):
        part = final[a].at[pl.ds(j * CAP, CAP), mine]
        core[a, j] = start(remote(part, part, core_send.at[a, j], core_recv.at[a, j], here.other_core()))

    far = {}

    def pick(a, i):
        if i >= 3:
            hop[a, i].wait_recv()
        block = source[a] if i == 0 else comp.at[a, i - 1]
        meta = metas[i]
        slots = slots_of(here, i)
        table = plain_table(meta, slots).astype(BF)
        weight = jnp.sum(gate_table(meta, slots), axis=1, keepdims=True) if a else None
        places = [5 + i] + (far_places(i) if i >= 3 else [])

        @pl.loop(0, HALF // COL)
        def _(c):
            cols = pl.ds(pl.multiple_of(c * COL, COL), COL)
            part = jnp.dot(table, block[:, cols], preferred_element_type=F32)
            if a:
                part = part * weight
            part = part.astype(BF)
            home = pl.ds(pl.multiple_of(here.core * HALF + c * COL, COL), COL)
            final[a][pl.ds(i * CAP, CAP), home] = part[:CAP]
            for n, j in enumerate(places):
                sendb[a, j - 5, :, cols] = part[(n + 1) * CAP : (n + 2) * CAP]

        way = STEPS[i][1]
        order = places[1:] + places[:1]
        for j in order:
            if j < 10:
                peer = here.near(1, 0)
            else:
                peer = far_peer(here, way, places.index(j) - 1, 1)
            far[a, j] = start(
                remote(
                    sendb.at[a, j - 5], final[a].at[pl.ds(j * CAP, CAP), mine],
                    far_send.at[a, j - 5], far_recv.at[a, j - 5], peer,
                )
            )
        to_core(a, i)

    metas_done = [False]

    def need_metas():
        if not metas_done[0]:
            for copy in started[:4]:
                copy.wait_recv()
            metas_done[0] = True

    first_hop(0)
    pick(0, 0)
    second_hop(0, 1)
    second_hop(0, 2)
    first_hop(1)
    need_metas()
    pick(0, 1)
    pick(0, 2)
    pick(1, 0)
    pick(0, 3)
    pick(0, 4)
    second_hop(1, 1)
    second_hop(1, 2)
    pick(1, 1)
    pick(1, 2)
    for j in (5, 6, 7, 8, 9, 10, 11, 12, 13, 14, 15):
        far[0, j].wait_recv()
        to_core(0, j)
    pick(1, 3)
    pick(1, 4)
    for j in (5, 6, 7, 8, 9, 10, 11, 12, 13, 14, 15):
        far[1, j].wait_recv()
        to_core(1, j)
    for a in range(2):
        for j in range(16):
            core[a, j].wait_recv()
    for copy in started:
        copy.wait_send()


def dispatch(routes, gates, place, tok, cot):
    vmem = pl.BlockSpec(memory_space=pltpu.VMEM)
    dma = pltpu.SemaphoreType.DMA
    return pl.pallas_call(
        dispatch_kernel,
        out_shape=(
            jax.ShapeDtypeStruct((ROWS, FULL), BF),
            jax.ShapeDtypeStruct((ROWS, FULL), BF),
            jax.ShapeDtypeStruct((5, 8, TOK), F32),
        ),
        in_specs=[vmem] * 5,
        out_specs=(vmem, vmem, vmem),
        scratch_shapes=[
            pltpu.VMEM((2, 4, TOK, HALF), BF),
            pltpu.VMEM((2, 11, CAP, HALF), BF),
            dma((4,)), dma((4,)),
            dma((2, 4)), dma((2, 4)),
            dma((2, 11)), dma((2, 11)),
            dma((2, 16)), dma((2, 16)),
        ],
        compiler_params=pltpu.CompilerParams(
            collective_id=1, has_side_effects=True, vmem_limit_bytes=40 * MIB
        ),
        name="dispatch",
    )(routes, gates, place, tok, cot)


def combine_kernel(
    part_out, part_in, term_gate, term_up, term_down, metas,
    mixed, input_grad, sum_gate, sum_up, sum_down,
    back, beside, distant, two, one, got_two, got_one,
    gu_first, gu_own, gu_mid, gu_home, gu_cross, gu_got,
    dn_first, dn_own, dn_mid, dn_home, dn_cross, dn_got,
    core_send, core_recv, side_send, side_recv, far_send, far_recv, tree_send, tree_recv,
    ring_send, ring_recv, plain_send, plain_recv, mid_send, mid_recv, cross_send, cross_recv, own_sem, home_sem,
):
    here = Place()
    barrier(tree_peers(here) + [here.along_y(1), here.along_y(-1), here.other_xh()])
    started = []

    def start(copy):
        copy.start()
        started.append(copy)
        return copy

    parts = (part_out, part_in)
    theirs = pl.ds(pl.multiple_of((1 - here.core) * HALF, HALF), HALF)
    spans = ((10 * CAP, 6 * CAP), (0, 10 * CAP))
    core = {}
    for a in range(2):
        for n, (at, size) in enumerate(spans):
            core[a, n] = start(
                remote(
                    parts[a].at[pl.ds(at, size), theirs], back.at[a, pl.ds(at, size)],
                    core_send.at[a, n], core_recv.at[a, n], here.other_core(),
                )
            )

    terms = (term_gate, term_up, term_down)
    sums = (sum_gate, sum_up, sum_down)

    def share(p, chunk, half):
        at = pl.ds(pl.multiple_of(chunk * 1024 + half * 512, 512), 512)
        return terms[p].at[:, at] if p == 2 else terms[p].at[at, :]

    def buf(p, gu, dn, *index):
        if p == 2:
            return dn.at[index] if index else dn
        return gu.at[(p,) + index]

    chunk_of = [lax.rem(here.y + 1, 4), lax.rem(here.y + 3, 4)]
    opposite = lax.rem(here.y + 2, 4)
    step = (1, -1)
    ring, plain, mid, cross, own, home = {}, {}, {}, {}, {}, {}
    for p in range(3):
        for w in range(2):
            ring[p, w] = start(
                remote(
                    share(p, opposite, w), buf(p, gu_first, dn_first, w),
                    ring_send.at[p, w], ring_recv.at[p, w], here.along_y(step[w]),
                )
            )
    for p in range(3):
        for w in range(2):
            plain[p, w] = start(
                remote(
                    share(p, chunk_of[w], 1 - w), buf(p, gu_mid, dn_mid, w, 1 - w),
                    plain_send.at[p, w], plain_recv.at[p, w], here.along_y(step[w]),
                )
            )
    for p in range(3):
        for w in range(2):
            own[p, w] = pltpu.make_async_copy(
                share(p, chunk_of[w], w), buf(p, gu_own, dn_own, w), own_sem.at[p, w]
            )
            own[p, w].start()
        for h in range(2):
            home[p, h] = pltpu.make_async_copy(
                share(p, here.y, h), buf(p, gu_home, dn_home, h), home_sem.at[p, h]
            )
            home[p, h].start()

    def by_rows(p, body):
        height = 64

        @pl.loop(0, (FF if p == 2 else 512) // height)
        def _(r):
            body(pl.ds(pl.multiple_of(r * height, height), height))

    def ring_step(p):
        for w in range(2):
            own[p, w].wait()
            ring[p, w].wait_recv()
            a, b = buf(p, gu_own, dn_own, w), buf(p, gu_first, dn_first, w)

            def body(r, a=a, b=b):
                a[r, :] = (a[r, :].astype(F32) + b[r, :].astype(F32)).astype(BF)

            by_rows(p, body)
            mid[p, w] = start(
                remote(
                    a, buf(p, gu_mid, dn_mid, w, w), mid_send.at[p, w], mid_recv.at[p, w],
                    here.along_y(step[w]),
                )
            )

    def cross_step(p):
        for w in range(2):
            home[p, w].wait()
            plain[p, w].wait_recv()
            mid[p, w].wait_recv()
        away = 1 - here.xh
        a, b, c = buf(p, gu_home, dn_home, away), buf(p, gu_mid, dn_mid, 0, away), buf(p, gu_mid, dn_mid, 1, away)
        d = buf(p, gu_cross, dn_cross)

        def body(r):
            d[r, :] = (a[r, :].astype(F32) + b[r, :].astype(F32) + c[r, :].astype(F32)).astype(BF)

        by_rows(p, body)
        cross[p] = start(
            remote(d, buf(p, gu_got, dn_got), cross_send.at[p], cross_recv.at[p], here.other_xh())
        )

    def last_step(p):
        cross[p].wait_recv()
        a = buf(p, gu_home, dn_home, here.xh)
        b, c = buf(p, gu_mid, dn_mid, 0, here.xh), buf(p, gu_mid, dn_mid, 1, here.xh)
        d = buf(p, gu_got, dn_got)
        out = sums[p]

        def body(r):
            total = a[r, :].astype(F32) + b[r, :].astype(F32) + c[r, :].astype(F32) + d[r, :].astype(F32)
            out[r, :] = total.astype(BF)

        by_rows(p, body)

    def add_halves(a, n):
        core[a, n].wait_recv()
        at, size = spans[n]

        @pl.loop(0, size // CAP)
        def _(r):
            rows = pl.ds(pl.multiple_of(at + r * CAP, CAP), CAP)

            @pl.loop(0, HALF // COL)
            def _(c):
                cols = pl.ds(pl.multiple_of(c * COL, COL), COL)
                own_cols = pl.ds(pl.multiple_of(here.core * HALF + c * COL, COL), COL)
                total = parts[a][rows, own_cols].astype(F32) + back[a, rows, cols].astype(F32)
                back[a, rows, cols] = total.astype(BF)

    side, far, tree = {}, {}, {}

    def send_rows(a):
        add_halves(a, 0)
        for way in (1, -1):
            for n in range(3):
                w = 0 if way == 1 else 1
                j = FAR[(way, n)]
                far[a, w, n] = start(
                    remote(
                        back.at[a, pl.ds(j * CAP, CAP)], distant.at[a, w, n],
                        far_send.at[a, w, n], far_recv.at[a, w, n], far_peer(here, way, n, -1),
                    )
                )
        add_halves(a, 1)
        for i in (3, 4, 1, 2, 0):
            side[a, i] = start(
                remote(
                    back.at[a, pl.ds((5 + i) * CAP, CAP)], beside.at[a, i],
                    side_send.at[a, i], side_recv.at[a, i], here.near(1, 0),
                )
            )

    def spread(a, i, more, out):
        side[a, i].wait_recv()
        meta = metas[i]
        slots = slots_of(here, i)
        if a:
            tables = [plain_table(meta, slots).astype(BF)]
        else:
            exact = gate_table(meta, slots)
            high = exact.astype(BF)
            tables = [high, (exact - high.astype(F32)).astype(BF)]

        @pl.loop(0, HALF // COL)
        def _(c):
            cols = pl.ds(pl.multiple_of(c * COL, COL), COL)
            rows = [back[a, pl.ds(i * CAP, CAP), cols], beside[a, i, :, cols]]
            if i >= 3:
                rows += [distant[a, i - 3, n, :, cols] for n in range(3)]
            rows = jnp.concatenate(rows, axis=0)
            total = None
            for table in tables:
                term = lax.dot_general(table, rows, (((0,), (0,)), ((), ())), preferred_element_type=F32)
                total = term if total is None else total + term
            for ref in more:
                total = total + ref[:, cols].astype(F32)
            out[:, cols] = total.astype(BF)

    def sum_two(a):
        for w in range(2):
            for n in range(3):
                far[a, w, n].wait_recv()
            spread(a, 3 + w, [], two.at[a, w])
            tree[a, w] = start(
                remote(
                    two.at[a, w], got_two.at[a, w], tree_send.at[a, w], tree_recv.at[a, w], here.near(0, -step[w])
                )
            )

    def sum_one(a):
        for w in range(2):
            tree[a, w].wait_recv()
            spread(a, 1 + w, [got_two.at[a, w]], one.at[a, w])
            tree[a, 2 + w] = start(
                remote(
                    one.at[a, w], got_one.at[a, w], tree_send.at[a, 2 + w], tree_recv.at[a, 2 + w],
                    here.near(0, -step[w]),
                )
            )

    def sum_home(a, out):
        for w in range(2):
            tree[a, 2 + w].wait_recv()
        spread(a, 0, [got_one.at[a, 0], got_one.at[a, 1]], out)

    send_rows(0)
    send_rows(1)
    ring_step(0)
    sum_two(0)
    ring_step(1)
    sum_two(1)
    ring_step(2)
    sum_one(0)
    sum_one(1)
    cross_step(0)
    sum_home(0, mixed)
    cross_step(1)
    sum_home(1, input_grad)
    last_step(0)
    cross_step(2)
    last_step(1)
    last_step(2)
    for copy in started:
        copy.wait_send()


def combine(part_out, part_in, term_gate, term_up, term_down, metas):
    vmem = pl.BlockSpec(memory_space=pltpu.VMEM)
    hbm = pl.BlockSpec(memory_space=pl.ANY)
    dma = pltpu.SemaphoreType.DMA
    return pl.pallas_call(
        combine_kernel,
        out_shape=(
            jax.ShapeDtypeStruct((TOK, HALF), BF),
            jax.ShapeDtypeStruct((TOK, HALF), BF),
            jax.ShapeDtypeStruct((512, FF), BF),
            jax.ShapeDtypeStruct((512, FF), BF),
            jax.ShapeDtypeStruct((FF, 512), BF),
        ),
        in_specs=[vmem, vmem, hbm, hbm, hbm, vmem],
        out_specs=(vmem,) * 5,
        scratch_shapes=[
            pltpu.VMEM((2, ROWS, HALF), BF),
            pltpu.VMEM((2, 5, CAP, HALF), BF),
            pltpu.VMEM((2, 2, 3, CAP, HALF), BF),
            pltpu.VMEM((2, 2, TOK, HALF), BF),
            pltpu.VMEM((2, 2, TOK, HALF), BF),
            pltpu.VMEM((2, 2, TOK, HALF), BF),
            pltpu.VMEM((2, 2, TOK, HALF), BF),
            pltpu.VMEM((2, 2, 512, FF), BF),
            pltpu.VMEM((2, 2, 512, FF), BF),
            pltpu.VMEM((2, 2, 2, 512, FF), BF),
            pltpu.VMEM((2, 2, 512, FF), BF),
            pltpu.VMEM((2, 512, FF), BF),
            pltpu.VMEM((2, 512, FF), BF),
            pltpu.VMEM((2, FF, 512), BF),
            pltpu.VMEM((2, FF, 512), BF),
            pltpu.VMEM((2, 2, FF, 512), BF),
            pltpu.VMEM((2, FF, 512), BF),
            pltpu.VMEM((FF, 512), BF),
            pltpu.VMEM((FF, 512), BF),
            dma((2, 2)), dma((2, 2)),
            dma((2, 5)), dma((2, 5)),
            dma((2, 2, 3)), dma((2, 2, 3)),
            dma((2, 4)), dma((2, 4)),
            dma((3, 2)), dma((3, 2)),
            dma((3, 2)), dma((3, 2)),
            dma((3, 2)), dma((3, 2)),
            dma((3,)), dma((3,)),
            dma((3, 2)), dma((3, 2)),
        ],
        compiler_params=pltpu.CompilerParams(
            collective_id=2, has_side_effects=True, vmem_limit_bytes=56 * MIB
        ),
        name="combine",
    )(part_out, part_in, term_gate, term_up, term_down, metas)


def per_device(tokens, routes, gates, dropped, placement, w_gate, w_up, w_down, cotangent):
    table = jnp.concatenate([routes.T, dropped.T], axis=0)
    place = jnp.broadcast_to(jnp.pad(placement, (0, 1))[:, None], (16, TOK))
    rows, grads, metas = dispatch(table, gates.T, place, tokens, cotangent)
    gate_matrix, up_matrix, down_matrix = w_gate[0], w_up[0], w_down[0]
    gate_pre = jnp.dot(rows, gate_matrix, preferred_element_type=F32)
    up_pre = jnp.dot(rows, up_matrix, preferred_element_type=F32)
    sigmoid_gate = jax.nn.sigmoid(gate_pre)
    silu_gate = gate_pre * sigmoid_gate
    hidden = (silu_gate * up_pre).astype(BF)
    part_out = jnp.dot(hidden, down_matrix, preferred_element_type=F32).astype(BF)
    contract = (((1,), (1,)), ((), ()))
    grad_hidden = lax.dot_general(grads, down_matrix, contract, preferred_element_type=F32)
    slope = sigmoid_gate * (1.0 + gate_pre * (1.0 - sigmoid_gate))
    grad_gate_pre = (grad_hidden * up_pre * slope).astype(BF)
    grad_up_pre = (grad_hidden * silu_gate).astype(BF)
    part_in = lax.dot_general(grad_gate_pre, gate_matrix, contract, preferred_element_type=F32)
    part_in = part_in + lax.dot_general(grad_up_pre, up_matrix, contract, preferred_element_type=F32)
    along_rows = (((0,), (0,)), ((), ()))
    term_gate = lax.dot_general(rows, grad_gate_pre, along_rows, preferred_element_type=F32).astype(BF)
    term_up = lax.dot_general(rows, grad_up_pre, along_rows, preferred_element_type=F32).astype(BF)
    term_down = lax.dot_general(hidden, grads, along_rows, preferred_element_type=F32).astype(BF)
    mixed, input_grad, grad_gate, grad_up, grad_down = combine(
        part_out, part_in.astype(BF), term_gate, term_up, term_down, metas
    )
    return mixed, input_grad, grad_gate[None], grad_up[None], grad_down[None]


def solution(mesh):
    in_specs = (
        P(("dp", "expert"), "tensor"),
        P(("dp", "expert"), None),
        P(("dp", "expert"), None),
        P(("dp", "expert"), None),
        P(),
        P("expert", None, "tensor"),
        P("expert", None, "tensor"),
        P("expert", "tensor", None),
        P(("dp", "expert"), "tensor"),
    )
    out_specs = (
        P(("dp", "expert"), "tensor"),
        P(("dp", "expert"), "tensor"),
        P("expert", "dp", "tensor"),
        P("expert", "dp", "tensor"),
        P("expert", "tensor", "dp"),
    )
    return jax.shard_map(
        per_device, mesh=mesh, in_specs=in_specs, out_specs=out_specs, check_vma=False
    )
```

```python
import jax
import jax.numpy as jnp
from jax import lax
from jax.experimental import pallas as pl
from jax.experimental.pallas import tpu as pltpu
from jax.sharding import PartitionSpec as P

MESH = pl.DeviceIdType.MESH
BF = jnp.bfloat16
F32 = jnp.float32
TOK = 128
CAP = 32
ROWS = 16 * CAP
FULL = 4096
HALF = 2048
FF = 384
COL = 512
MIB = 1 << 20

STEPS = ((0, 0), (1, 1), (1, -1), (2, 1), (2, -1))
FAR = {(1, 0): 10, (1, 1): 11, (-1, 0): 12, (-1, 1): 13, (1, 2): 14, (-1, 2): 15}


class Place:
    def __init__(self):
        self.dp = lax.axis_index("dp")
        expert = lax.axis_index("expert")
        self.core = lax.axis_index("tensor")
        self.y = lax.div(self.dp, 2)
        self.xh = lax.rem(self.dp, 2)
        self.x = lax.div(expert, 8)
        self.z = lax.rem(expert, 8)

    def slot(self, dx, dz):
        return lax.rem(self.x + dx, 2) * 8 + lax.rem(self.z + dz + 8, 8)

    def near(self, dx, dz):
        return (self.dp, self.slot(dx, dz), self.core)

    def other_core(self):
        return (self.dp, self.slot(0, 0), 1 - self.core)

    def along_y(self, dy):
        return (lax.rem(self.y + dy + 4, 4) * 2 + self.xh, self.slot(0, 0), self.core)

    def other_xh(self):
        return (self.y * 2 + 1 - self.xh, self.slot(0, 0), self.core)


def barrier(peers):
    sem = pltpu.get_barrier_semaphore()
    for peer in peers:
        pl.semaphore_signal(sem, inc=1, device_id=peer, device_id_type=MESH)
    pl.semaphore_wait(sem, len(peers))


def tree_peers(here):
    return [
        here.near(0, 1), here.near(0, -1), here.near(0, 2), here.near(0, -2), here.near(1, 0),
        here.near(1, 1), here.near(1, -1), here.near(1, 2), here.near(1, -2), here.other_core(),
    ]


def remote(src, dst, send, recv, peer):
    return pltpu.make_async_remote_copy(
        src_ref=src, dst_ref=dst, send_sem=send, recv_sem=recv, device_id=peer, device_id_type=MESH
    )


def slots_of(here, index):
    slots = [here.slot(0, 0), here.slot(1, 0)]
    depth, way = STEPS[index]
    if depth == 2:
        slots += [here.slot(0, way), here.slot(1, way)]
        slots.append(here.slot(0, 2) if way == 1 else here.slot(1, -2))
    return slots


def far_places(index):
    way = STEPS[index][1]
    return [FAR[(way, n)] for n in range(3)]


def far_peer(here, way, n, sign):
    if n == 0:
        return here.near(0, way * sign)
    if n == 1:
        return here.near(1, way * sign)
    return here.near(0, 2 * sign) if way == 1 else here.near(1, -2 * sign)


def hits(meta, slots):
    ids = jnp.concatenate(
        [(s * CAP + lax.broadcasted_iota(jnp.int32, (CAP, TOK), 0)).astype(F32) for s in slots], axis=0
    )
    return meta[0:1, :] == ids, meta[1:2, :] == ids


def plain_table(meta, slots):
    first, second = hits(meta, slots)
    return jnp.where(first | second, 1.0, 0.0).astype(F32)


def gate_table(meta, slots):
    first, second = hits(meta, slots)
    return jnp.where(first, meta[2:3, :], 0.0) + jnp.where(second, meta[3:4, :], 0.0)


def make_meta(routes, gates, dropped, placement):
    row = lax.broadcasted_iota(jnp.int32, (TOK, TOK), 0)
    column = lax.broadcasted_iota(jnp.int32, (TOK, TOK), 1)
    route = [routes[k : k + 1, :] for k in range(2)]
    kept = [dropped[k : k + 1, :] == 0 for k in range(2)]
    gate = [gates[k : k + 1, :] for k in range(2)]
    label = lax.broadcasted_iota(jnp.int32, (16, TOK), 0)
    base = jnp.zeros((16, TOK), F32)
    for e in range(15):
        base = jnp.where(label == e, (placement[e] * CAP).astype(F32), base)
    hit = [jnp.where((route[k] == label) & kept[k], 1.0, 0.0).astype(F32) for k in range(2)]
    before = jnp.dot(
        (hit[0] + hit[1]).astype(BF), jnp.where(row < column, 1.0, 0.0).astype(BF), preferred_element_type=F32
    )
    at = [
        jnp.sum(hit[0] * (before + base), axis=0, keepdims=True),
        jnp.sum(hit[1] * (before + hit[0] + base), axis=0, keepdims=True),
    ]
    out = [jnp.where(kept[k], at[k], -1.0) for k in range(2)]
    out += [jnp.where(kept[k], gate[k], 0.0) for k in range(2)]
    out.append(jnp.zeros((4, TOK), F32))
    return jnp.concatenate(out, axis=0)


NT = (((1,), (1,)), ((), ()))


def layer_kernel(
    tok, cot, routes, gates, dropped, placement, w_gate, w_up, w_down,
    mixed, input_grad, sum_gate, sum_up, sum_down,
    tokv, cotv, metas, comp, sendb, rows_tok, rows_cot, wide, down, pre, hidden, slopes, terms,
    back, beside, distant, got_two, got_one, first, middle, got,
    meta_send, meta_recv, hop_send, hop_recv, row_send, row_recv, pair_send, pair_recv,
    core_send, core_recv, side_send, side_recv, far_send, far_recv, tree_send, tree_recv,
    ring_send, ring_recv, plain_send, plain_recv, mid_send, mid_recv, cross_send, cross_recv, load_sem,
):
    here = Place()
    waiting = []

    def start(copy):
        copy.start()
        waiting.append(copy)
        return copy

    def sent(copy):
        waiting[:] = [other for other in waiting if other is not copy]
        copy.wait_send()

    loads = [
        pltpu.make_async_copy(tok, tokv, load_sem.at[0]),
        pltpu.make_async_copy(cot, cotv, load_sem.at[1]),
        pltpu.make_async_copy(w_gate, wide.at[:, pl.ds(0, FF)], load_sem.at[2]),
        pltpu.make_async_copy(w_up, wide.at[:, pl.ds(FF, FF)], load_sem.at[3]),
        pltpu.make_async_copy(w_down, down, load_sem.at[4]),
    ]
    barrier(tree_peers(here) + [here.along_y(1), here.along_y(-1), here.other_xh()])
    loads[0].start()

    source = (tok, cot)
    local = (tokv, cotv)
    final = (rows_tok, rows_cot)
    mine = pl.ds(pl.multiple_of(here.core * HALF, HALF), HALF)
    theirs = pl.ds(pl.multiple_of((1 - here.core) * HALF, HALF), HALF)
    hop, row, pair = {}, {}, {}

    def first_hop(a):
        for i in (1, 2):
            hop[a, i] = start(
                remote(source[a], comp.at[a, i - 1], hop_send.at[a, i - 1], hop_recv.at[a, i - 1], here.near(0, STEPS[i][1]))
            )

    def second_hop(a):
        for i in (1, 2):
            hop[a, i].wait_recv()
            hop[a, i + 2] = start(
                remote(comp.at[a, i - 1], comp.at[a, i + 1], hop_send.at[a, i + 1], hop_recv.at[a, i + 1], here.near(0, STEPS[i][1]))
            )

    def to_core(a, j):
        part = final[a].at[pl.ds(j * CAP, CAP), mine]
        pair[a, j] = start(remote(part, part, pair_send.at[a, j], pair_recv.at[a, j], here.other_core()))

    def pick(a, i):
        if i >= 3:
            hop[a, i].wait_recv()
        block = local[a] if i == 0 else comp.at[a, i - 1]
        meta = metas[i]
        slots = slots_of(here, i)
        table = plain_table(meta, slots).astype(BF)
        weight = jnp.sum(gate_table(meta, slots), axis=1, keepdims=True) if a else None
        places = [5 + i] + (far_places(i) if i >= 3 else [])

        @pl.loop(0, HALF // COL)
        def _(c):
            cols = pl.ds(pl.multiple_of(c * COL, COL), COL)
            part = jnp.dot(table, block[:, cols], preferred_element_type=F32)
            if a:
                part = part * weight
            part = part.astype(BF)
            home = pl.ds(pl.multiple_of(here.core * HALF + c * COL, COL), COL)
            final[a][pl.ds(i * CAP, CAP), home] = part[:CAP]
            for n, j in enumerate(places):
                sendb[a, j - 5, :, cols] = part[(n + 1) * CAP : (n + 2) * CAP]

        way = STEPS[i][1]
        for j in places[1:] + places[:1]:
            peer = here.near(1, 0) if j < 10 else far_peer(here, way, places.index(j) - 1, 1)
            row[a, j] = start(
                remote(
                    sendb.at[a, j - 5], final[a].at[pl.ds(j * CAP, CAP), mine],
                    row_send.at[a, j - 5], row_recv.at[a, j - 5], peer,
                )
            )
        to_core(a, i)

    def collect(a):
        for j in (5, 6, 7, 8, 9, 10, 11, 12, 13, 14, 15):
            row[a, j].wait_recv()
            to_core(a, j)

    def whole(a):
        for j in range(16):
            pair[a, j].wait_recv()

    def forward(r):
        rows = pl.ds(r * 256, 256)

        @pl.loop(0, 3)
        def _(c):
            cols = pl.ds(pl.multiple_of(c * 256, 256), 256)
            pre[rows, cols] = jnp.dot(rows_tok[rows, :], wide[:, cols], preferred_element_type=F32)

    def activate():
        @pl.loop(0, ROWS // 64)
        def _(r):
            rows = pl.ds(pl.multiple_of(r * 64, 64), 64)
            gate = pre[rows, :FF]
            hidden[rows, :] = (gate * jax.nn.sigmoid(gate) * pre[rows, FF:]).astype(BF)

    def forward_out():
        @pl.loop(0, FULL // 256)
        def _(c):
            cols = pl.ds(pl.multiple_of(c * 256, 256), 256)
            terms[pl.ds(0, ROWS), cols] = jnp.dot(
                hidden[...], down[:, cols], preferred_element_type=F32
            ).astype(BF)

    def backward_hidden():
        @pl.loop(0, 4)
        def _(r):
            rows = pl.ds(pl.multiple_of(r * 128, 128), 128)
            grad = lax.dot_general(rows_cot[rows, :], down[...], NT, preferred_element_type=F32)
            gate, up = pre[rows, :FF], pre[rows, FF:]
            sigmoid = jax.nn.sigmoid(gate)
            slope = sigmoid * (1.0 + gate * (1.0 - sigmoid))
            slopes[rows, :FF] = (grad * up * slope).astype(BF)
            slopes[rows, FF:] = (grad * (gate * sigmoid)).astype(BF)

    def backward_rows():
        both = slopes[...]

        @pl.loop(0, FULL // 256)
        def _(c):
            cols = pl.ds(pl.multiple_of(c * 256, 256), 256)
            rows_tok[:, cols] = lax.dot_general(both, wide[cols, :], NT, preferred_element_type=F32).astype(BF)

    chunk_of = [lax.rem(here.y + 1, 4), lax.rem(here.y + 3, 4)]
    opposite = lax.rem(here.y + 2, 4)
    step = (1, -1)
    sums = (sum_gate, sum_up, sum_down)
    ring, plain, mid, cross = {}, {}, {}, {}

    def share(p, chunk, half):
        return terms.at[pl.ds(p * FF, FF), pl.ds(pl.multiple_of(chunk * 1024 + half * 512, 512), 512)]

    def weight_terms(pieces, small, big):
        at, size = pieces[0] * FF, len(pieces) * FF
        turned = small[...].T

        def chunk_terms(chunk):
            @pl.loop(0, 4)
            def _(c):
                cols = pl.ds(pl.multiple_of(chunk * 1024 + c * 256, 256), 256)
                terms[pl.ds(at, size), cols] = jnp.dot(turned, big[:, cols], preferred_element_type=F32).astype(BF)

        chunk_terms(opposite)
        for p in pieces:
            for w in range(2):
                ring[p, w] = start(
                    remote(
                        share(p, opposite, w), first.at[p, w],
                        ring_send.at[p, w], ring_recv.at[p, w], here.along_y(step[w]),
                    )
                )
        chunk_terms(chunk_of[0])
        chunk_terms(chunk_of[1])
        for p in pieces:
            for w in range(2):
                plain[p, w] = start(
                    remote(
                        share(p, chunk_of[w], 1 - w), middle.at[p, w, 1 - w],
                        plain_send.at[p, w], plain_recv.at[p, w], here.along_y(step[w]),
                    )
                )
        chunk_terms(here.y)

    def by_rows(body, height=64):
        @pl.loop(0, FF // height)
        def _(r):
            body(pl.ds(pl.multiple_of(r * height, height), height))

    def ring_step(p):
        for w in range(2):
            ring[p, w].wait_recv()
            a, b = share(p, chunk_of[w], w), first.at[p, w]

            def body(r, a=a, b=b):
                a[r, :] = (a[r, :].astype(F32) + b[r, :].astype(F32)).astype(BF)

            by_rows(body)
            mid[p, w] = start(
                remote(a, middle.at[p, w, w], mid_send.at[p, w], mid_recv.at[p, w], here.along_y(step[w]))
            )

    def cross_step(p):
        for w in range(2):
            plain[p, w].wait_recv()
            mid[p, w].wait_recv()
        away = 1 - here.xh
        a, b, c = share(p, here.y, away), middle.at[p, 0, away], middle.at[p, 1, away]

        def body(r):
            a[r, :] = (a[r, :].astype(F32) + b[r, :].astype(F32) + c[r, :].astype(F32)).astype(BF)

        by_rows(body)
        cross[p] = start(remote(a, got.at[p], cross_send.at[p], cross_recv.at[p], here.other_xh()))

    def last_step(p):
        cross[p].wait_recv()
        a, b, c = share(p, here.y, here.xh), middle.at[p, 0, here.xh], middle.at[p, 1, here.xh]
        for n in range(3):
            r = pl.ds(n * 128, 128)
            total = a[r, :].astype(F32) + b[r, :].astype(F32) + c[r, :].astype(F32) + got[p, r, :].astype(F32)
            if p == 2:
                sums[p][r, :] = total.astype(BF)
            else:
                sums[p][:, r] = total.T.astype(BF)

    parts = (terms, rows_tok)
    spans = ((10 * CAP, 6 * CAP), (0, 10 * CAP))
    core, side, far, tree = {}, {}, {}, {}

    def swap_halves(a):
        for n, (at, size) in enumerate(spans):
            core[a, n] = start(
                remote(
                    parts[a].at[pl.ds(at, size), theirs], back.at[a, pl.ds(at, size)],
                    core_send.at[a, n], core_recv.at[a, n], here.other_core(),
                )
            )

    def add_halves(a, n):
        core[a, n].wait_recv()
        at, size = spans[n]

        @pl.loop(0, size // CAP)
        def _(r):
            rows = pl.ds(pl.multiple_of(at + r * CAP, CAP), CAP)
            total = parts[a][rows, mine].astype(F32) + back[a, rows, :].astype(F32)
            back[a, rows, :] = total.astype(BF)

    def send_rows(a):
        add_halves(a, 0)
        for w, way in enumerate(step):
            for n in range(3):
                far[a, w, n] = start(
                    remote(
                        back.at[a, pl.ds(FAR[(way, n)] * CAP, CAP)], distant.at[a, w, n],
                        far_send.at[a, w, n], far_recv.at[a, w, n], far_peer(here, way, n, -1),
                    )
                )
        add_halves(a, 1)
        for i in (3, 4, 1, 2, 0):
            side[a, i] = start(
                remote(
                    back.at[a, pl.ds((5 + i) * CAP, CAP)], beside.at[a, i],
                    side_send.at[a, i], side_recv.at[a, i], here.near(1, 0),
                )
            )

    def spread(a, i, more, out):
        side[a, i].wait_recv()
        meta = metas[i]
        slots = slots_of(here, i)
        if a:
            tables = [plain_table(meta, slots).astype(BF)]
        else:
            exact = gate_table(meta, slots)
            high = exact.astype(BF)
            tables = [high, (exact - high.astype(F32)).astype(BF)]

        @pl.loop(0, HALF // COL)
        def _(c):
            cols = pl.ds(pl.multiple_of(c * COL, COL), COL)
            rows = [back[a, pl.ds(i * CAP, CAP), cols], beside[a, i, :, cols]]
            if i >= 3:
                rows += [distant[a, i - 3, n, :, cols] for n in range(3)]
            rows = jnp.concatenate(rows, axis=0)
            total = None
            for table in tables:
                term = lax.dot_general(table, rows, (((0,), (0,)), ((), ())), preferred_element_type=F32)
                total = term if total is None else total + term
            for ref in more:
                total = total + ref[:, cols].astype(F32)
            out[:, cols] = total.astype(BF)

    def sum_two(a):
        for w in range(2):
            for n in range(3):
                far[a, w, n].wait_recv()
            spread(a, 3 + w, [], comp.at[a, w])
            tree[a, w] = start(
                remote(
                    comp.at[a, w], got_two.at[a, w], tree_send.at[a, w], tree_recv.at[a, w], here.near(0, -step[w])
                )
            )

    def sum_one(a):
        for w in range(2):
            tree[a, w].wait_recv()
            spread(a, 1 + w, [got_two.at[a, w]], comp.at[a, 2 + w])
            tree[a, 2 + w] = start(
                remote(
                    comp.at[a, 2 + w], got_one.at[a, w], tree_send.at[a, 2 + w], tree_recv.at[a, 2 + w],
                    here.near(0, -step[w]),
                )
            )

    def sum_home(a, out):
        for w in range(2):
            tree[a, 2 + w].wait_recv()
        spread(a, 0, [got_one.at[a, 0], got_one.at[a, 1]], out)

    first_hop(0)
    for load in loads[1:]:
        load.start()
    metas[0] = make_meta(routes[...], gates[...], dropped[...], placement)
    about = []
    for i in range(1, 5):
        depth, way = STEPS[i]
        about.append(
            start(remote(metas.at[0], metas.at[i], meta_send.at[i - 1], meta_recv.at[i - 1], here.near(0, way * depth)))
        )
    loads[0].wait()
    pick(0, 0)
    second_hop(0)
    first_hop(1)
    for copy in about:
        copy.wait_recv()
    pick(0, 1)
    pick(0, 2)
    loads[1].wait()
    pick(1, 0)
    pick(0, 3)
    pick(0, 4)
    second_hop(1)
    pick(1, 1)
    pick(1, 2)
    collect(0)
    for load in loads[2:]:
        load.wait()
    whole(0)
    forward(0)
    forward(1)
    pick(1, 3)
    pick(1, 4)
    activate()
    forward_out()
    swap_halves(0)
    collect(1)
    send_rows(0)
    whole(1)
    for i in range(1, 5):
        for a in range(2):
            sent(hop[a, i])
    for n in range(2):
        sent(core[0, n])
    for j in range(16):
        sent(pair[0, j])
    weight_terms((2,), hidden, rows_cot)
    backward_hidden()
    sum_two(0)
    weight_terms((0, 1), slopes, rows_tok)
    ring_step(2)
    sum_one(0)
    backward_rows()
    swap_halves(1)
    ring_step(0)
    send_rows(1)
    ring_step(1)
    sum_two(1)
    sum_home(0, mixed)
    cross_step(2)
    sum_one(1)
    cross_step(0)
    sum_home(1, input_grad)
    last_step(2)
    cross_step(1)
    last_step(0)
    last_step(1)
    for copy in waiting:
        copy.wait_send()


OUTS = ((TOK, HALF), (TOK, HALF), (512, FF), (512, FF), (FF, 512))


def layer(tok, cot, routes, gates, dropped, placement, w_gate, w_up, w_down):
    vmem = pl.BlockSpec(memory_space=pltpu.VMEM)
    hbm = pl.BlockSpec(memory_space=pl.ANY)
    smem = pl.BlockSpec(memory_space=pltpu.SMEM)
    dma = pltpu.SemaphoreType.DMA
    return pl.pallas_call(
        layer_kernel,
        out_shape=tuple(jax.ShapeDtypeStruct(shape, BF) for shape in OUTS),
        in_specs=[hbm, hbm, vmem, vmem, vmem, smem, hbm, hbm, hbm],
        out_specs=(vmem,) * 5,
        scratch_shapes=[
            pltpu.VMEM((TOK, HALF), BF),
            pltpu.VMEM((TOK, HALF), BF),
            pltpu.VMEM((5, 8, TOK), F32),
            pltpu.VMEM((2, 4, TOK, HALF), BF),
            pltpu.VMEM((2, 11, CAP, HALF), BF),
            pltpu.VMEM((ROWS, FULL), BF),
            pltpu.VMEM((ROWS, FULL), BF),
            pltpu.VMEM((FULL, 2 * FF), BF),
            pltpu.VMEM((FF, FULL), BF),
            pltpu.VMEM((ROWS, 2 * FF), F32),
            pltpu.VMEM((ROWS, FF), BF),
            pltpu.VMEM((ROWS, 2 * FF), BF),
            pltpu.VMEM((3 * FF, FULL), BF),
            pltpu.VMEM((2, ROWS, HALF), BF),
            pltpu.VMEM((2, 5, CAP, HALF), BF),
            pltpu.VMEM((2, 2, 3, CAP, HALF), BF),
            pltpu.VMEM((2, 2, TOK, HALF), BF),
            pltpu.VMEM((2, 2, TOK, HALF), BF),
            pltpu.VMEM((3, 2, FF, 512), BF),
            pltpu.VMEM((3, 2, 2, FF, 512), BF),
            pltpu.VMEM((3, FF, 512), BF),
            dma((4,)), dma((4,)),
            dma((2, 4)), dma((2, 4)),
            dma((2, 11)), dma((2, 11)),
            dma((2, 16)), dma((2, 16)),
            dma((2, 2)), dma((2, 2)),
            dma((2, 5)), dma((2, 5)),
            dma((2, 2, 3)), dma((2, 2, 3)),
            dma((2, 4)), dma((2, 4)),
            dma((3, 2)), dma((3, 2)),
            dma((3, 2)), dma((3, 2)),
            dma((3, 2)), dma((3, 2)),
            dma((3,)), dma((3,)),
            dma((5,)),
        ],
        compiler_params=pltpu.CompilerParams(
            collective_id=1, has_side_effects=True, vmem_limit_bytes=63 * MIB
        ),
        name="layer",
    )(tok, cot, routes, gates, dropped, placement, w_gate, w_up, w_down)


def finish_kernel(*refs):
    count = len(OUTS)
    held, load_sem, store_sem = refs[2 * count : 3 * count], refs[3 * count], refs[3 * count + 1]
    loads = [pltpu.make_async_copy(refs[i], held[i], load_sem.at[i]) for i in range(count)]
    stores = [pltpu.make_async_copy(held[i], refs[count + i], store_sem.at[i]) for i in range(count)]
    for load in loads:
        load.start()
    for load, store in zip(loads, stores):
        load.wait()
        store.start()
    for store in stores:
        store.wait()


def finish(*arrays):
    hbm = pl.BlockSpec(memory_space=pl.ANY)
    return pl.pallas_call(
        finish_kernel,
        out_shape=tuple(jax.ShapeDtypeStruct(shape, BF) for shape in OUTS),
        in_specs=[hbm] * len(OUTS),
        out_specs=(hbm,) * len(OUTS),
        scratch_shapes=[pltpu.VMEM(shape, BF) for shape in OUTS]
        + [pltpu.SemaphoreType.DMA((len(OUTS),))] * 2,
        name="finish",
    )(*arrays)


def per_device(tokens, routes, gates, dropped, placement, w_gate, w_up, w_down, cotangent):
    mixed, input_grad, grad_gate, grad_up, grad_down = finish(
        *layer(tokens, cotangent, routes.T, gates.T, dropped.T, placement, w_gate[0], w_up[0], w_down[0])
    )
    return mixed, input_grad, grad_gate[None], grad_up[None], grad_down[None]


def solution(mesh):
    in_specs = (
        P(("dp", "expert"), "tensor"),
        P(("dp", "expert"), None),
        P(("dp", "expert"), None),
        P(("dp", "expert"), None),
        P(),
        P("expert", None, "tensor"),
        P("expert", None, "tensor"),
        P("expert", "tensor", None),
        P(("dp", "expert"), "tensor"),
    )
    out_specs = (
        P(("dp", "expert"), "tensor"),
        P(("dp", "expert"), "tensor"),
        P("expert", "dp", "tensor"),
        P("expert", "dp", "tensor"),
        P("expert", "tensor", "dp"),
    )
    return jax.shard_map(
        per_device, mesh=mesh, in_specs=in_specs, out_specs=out_specs, check_vma=False
    )
```

```python
import jax
import jax.numpy as jnp
from jax import lax
from jax.experimental import pallas as pl
from jax.experimental.pallas import tpu as pltpu
from jax.sharding import PartitionSpec as P

MESH = pl.DeviceIdType.MESH
BF = jnp.bfloat16
F32 = jnp.float32
TOK = 128
CAP = 32
ROWS = 16 * CAP
FULL = 4096
HALF = 2048
FF = 384
COL = 512
MIB = 1 << 20

STEPS = ((0, 0), (1, 1), (1, -1), (2, 1), (2, -1))
FAR = {(1, 0): 10, (1, 1): 11, (-1, 0): 12, (-1, 1): 13, (1, 2): 14, (-1, 2): 15}


class Place:
    def __init__(self):
        self.dp = lax.axis_index("dp")
        expert = lax.axis_index("expert")
        self.core = lax.axis_index("tensor")
        self.y = lax.div(self.dp, 2)
        self.xh = lax.rem(self.dp, 2)
        self.x = lax.div(expert, 8)
        self.z = lax.rem(expert, 8)

    def slot(self, dx, dz):
        return lax.rem(self.x + dx, 2) * 8 + lax.rem(self.z + dz + 8, 8)

    def near(self, dx, dz):
        return (self.dp, self.slot(dx, dz), self.core)

    def other_core(self):
        return (self.dp, self.slot(0, 0), 1 - self.core)

    def along_y(self, dy):
        return (lax.rem(self.y + dy + 4, 4) * 2 + self.xh, self.slot(0, 0), self.core)

    def twin(self):
        y = self.y + 1 - 2 * lax.rem(self.y, 2)
        return (y * 2 + self.xh, self.slot(0, 0), self.core)

    def mate(self):
        return ((3 - self.y) * 2 + self.xh, self.slot(0, 0), self.core)

    def other_xh(self):
        return (self.y * 2 + 1 - self.xh, self.slot(0, 0), self.core)


def barrier(peers):
    sem = pltpu.get_barrier_semaphore()
    for peer in peers:
        pl.semaphore_signal(sem, inc=1, device_id=peer, device_id_type=MESH)
    pl.semaphore_wait(sem, len(peers))


def tree_peers(here):
    return [
        here.near(0, 1), here.near(0, -1), here.near(0, 2), here.near(0, -2), here.near(1, 0),
        here.near(1, 1), here.near(1, -1), here.near(1, 2), here.near(1, -2), here.other_core(),
    ]


def remote(src, dst, send, recv, peer):
    return pltpu.make_async_remote_copy(
        src_ref=src, dst_ref=dst, send_sem=send, recv_sem=recv, device_id=peer, device_id_type=MESH
    )


def slots_of(here, index):
    slots = [here.slot(0, 0), here.slot(1, 0)]
    depth, way = STEPS[index]
    if depth == 2:
        slots += [here.slot(0, way), here.slot(1, way)]
        slots.append(here.slot(0, 2) if way == 1 else here.slot(1, -2))
    return slots


def far_places(index):
    way = STEPS[index][1]
    return [FAR[(way, n)] for n in range(3)]


def far_peer(here, way, n, sign):
    if n == 0:
        return here.near(0, way * sign)
    if n == 1:
        return here.near(1, way * sign)
    return here.near(0, 2 * sign) if way == 1 else here.near(1, -2 * sign)


def hits(meta, slots):
    ids = jnp.concatenate(
        [(s * CAP + lax.broadcasted_iota(jnp.int32, (CAP, TOK), 0)).astype(F32) for s in slots], axis=0
    )
    return meta[0:1, :] == ids, meta[1:2, :] == ids


def plain_table(meta, slots):
    first, second = hits(meta, slots)
    return jnp.where(first | second, 1.0, 0.0).astype(F32)


def gate_table(meta, slots):
    first, second = hits(meta, slots)
    return jnp.where(first, meta[2:3, :], 0.0) + jnp.where(second, meta[3:4, :], 0.0)


def make_meta(routes, gates, dropped, placement):
    row = lax.broadcasted_iota(jnp.int32, (TOK, TOK), 0)
    column = lax.broadcasted_iota(jnp.int32, (TOK, TOK), 1)
    route = [routes[k : k + 1, :] for k in range(2)]
    kept = [dropped[k : k + 1, :] == 0 for k in range(2)]
    gate = [gates[k : k + 1, :] for k in range(2)]
    label = lax.broadcasted_iota(jnp.int32, (16, TOK), 0)
    base = jnp.zeros((16, TOK), F32)
    for e in range(15):
        base = jnp.where(label == e, (placement[e] * CAP).astype(F32), base)
    hit = [jnp.where((route[k] == label) & kept[k], 1.0, 0.0).astype(F32) for k in range(2)]
    before = jnp.dot(
        (hit[0] + hit[1]).astype(BF), jnp.where(row < column, 1.0, 0.0).astype(BF), preferred_element_type=F32
    )
    at = [
        jnp.sum(hit[0] * (before + base), axis=0, keepdims=True),
        jnp.sum(hit[1] * (before + hit[0] + base), axis=0, keepdims=True),
    ]
    out = [jnp.where(kept[k], at[k], -1.0) for k in range(2)]
    out += [jnp.where(kept[k], gate[k], 0.0) for k in range(2)]
    out.append(jnp.zeros((4, TOK), F32))
    return jnp.concatenate(out, axis=0)


NT = (((1,), (1,)), ((), ()))


def layer_kernel(
    tok, cot, routes, gates, dropped, placement, w_gate, w_up, w_down,
    mixed, input_grad, sum_gate, sum_up, sum_down,
    tokv, cotv, metas, comp, sendb, rows_tok, rows_cot, weights, down, pre, hidden, slopes, part_out,
    twin_tok, twin_slopes, term_wide, term_down,
    back, beside, distant, got_two, got_one, got_pair, got_wide, first_down, middle_down, got_down,
    meta_send, meta_recv, hop_send, hop_recv, row_send, row_recv, pair_send, pair_recv,
    core_send, core_recv, side_send, side_recv, far_send, far_recv, tree_send, tree_recv,
    ring_send, ring_recv, plain_send, plain_recv, mid_send, mid_recv, mate_send, mate_recv,
    cross_send, cross_recv, twin_send, twin_recv, load_sem,
):
    here = Place()
    waiting = []

    def start(copy):
        copy.start()
        waiting.append(copy)
        return copy

    def sent(copy):
        waiting[:] = [other for other in waiting if other is not copy]
        copy.wait_send()

    loads = [
        pltpu.make_async_copy(tok, tokv, load_sem.at[0]),
        pltpu.make_async_copy(cot, cotv, load_sem.at[1]),
        pltpu.make_async_copy(w_gate, weights.at[:, pl.ds(0, FF)], load_sem.at[2]),
        pltpu.make_async_copy(w_up, weights.at[:, pl.ds(FF, FF)], load_sem.at[3]),
        pltpu.make_async_copy(w_down, down, load_sem.at[4]),
    ]
    barrier(tree_peers(here) + [here.along_y(1), here.along_y(-1), here.other_xh()])
    loads[0].start()

    source = (tok, cot)
    local = (tokv, cotv)
    final = (rows_tok, rows_cot)
    mine = pl.ds(pl.multiple_of(here.core * HALF, HALF), HALF)
    theirs = pl.ds(pl.multiple_of((1 - here.core) * HALF, HALF), HALF)
    hop, row, pair = {}, {}, {}

    def hop_copy(a, i, h, block):
        cols = pl.ds(h * 1024, 1024)
        way = STEPS[i][1]
        hop[a, i, h] = start(
            remote(
                block.at[:, cols], comp.at[a, i - 1, :, cols],
                hop_send.at[a, i - 1, h], hop_recv.at[a, i - 1, h], here.near(0, way),
            )
        )

    def first_hop(a):
        for h in range(2):
            for i in (1, 2):
                hop_copy(a, i, h, source[a])

    def second_hop(a):
        for h in range(2):
            for i in (1, 2):
                hop[a, i, h].wait_recv()
                hop_copy(a, i + 2, h, comp.at[a, i - 1])

    def to_core(a, j):
        part = final[a].at[pl.ds(j * CAP, CAP), mine]
        pair[a, j] = start(remote(part, part, pair_send.at[a, j], pair_recv.at[a, j], here.other_core()))

    def pick(a, i):
        block = local[a] if i == 0 else comp.at[a, i - 1]
        meta = metas[i]
        slots = slots_of(here, i)
        table = plain_table(meta, slots).astype(BF)
        weight = jnp.sum(gate_table(meta, slots), axis=1, keepdims=True) if a else None
        places = [5 + i] + (far_places(i) if i >= 3 else [])

        def select(c):
            cols = pl.ds(pl.multiple_of(c * COL, COL), COL)
            part = jnp.dot(table, block[:, cols], preferred_element_type=F32)
            if a:
                part = part * weight
            part = part.astype(BF)
            home = pl.ds(pl.multiple_of(here.core * HALF + c * COL, COL), COL)
            final[a][pl.ds(i * CAP, CAP), home] = part[:CAP]
            for n, j in enumerate(places):
                sendb[a, j - 5, :, cols] = part[(n + 1) * CAP : (n + 2) * CAP]

        for h in range(2):
            if i >= 3 and (a or h):
                hop[a, i, h].wait_recv()
            pl.loop(2 * h, 2 * h + 2)(select)
        way = STEPS[i][1]
        for j in places[:0:-1] + places[:1]:
            peer = here.near(1, 0) if j < 10 else far_peer(here, way, places.index(j) - 1, 1)
            row[a, j] = start(
                remote(
                    sendb.at[a, j - 5], final[a].at[pl.ds(j * CAP, CAP), mine],
                    row_send.at[a, j - 5], row_recv.at[a, j - 5], peer,
                )
            )
        to_core(a, i)

    def collect(a):
        for j in range(5, 16):
            row[a, j].wait_recv()
            to_core(a, j)

    def whole(a):
        for j in range(16):
            pair[a, j].wait_recv()

    def forward(r):
        rows = pl.ds(r * 256, 256)

        @pl.loop(0, 3)
        def _(c):
            cols = pl.ds(pl.multiple_of(c * 256, 256), 256)
            pre[rows, cols] = jnp.dot(rows_tok[rows, :], weights[:, cols], preferred_element_type=F32)

    def activate():
        @pl.loop(0, ROWS // 64)
        def _(r):
            rows = pl.ds(pl.multiple_of(r * 64, 64), 64)
            gate = pre[rows, :FF]
            hidden[rows, :] = (gate * jax.nn.sigmoid(gate) * pre[rows, FF:]).astype(BF)

    def forward_out():
        @pl.loop(0, FULL // 256)
        def _(c):
            cols = pl.ds(pl.multiple_of(c * 256, 256), 256)
            part_out[:, cols] = jnp.dot(
                hidden[...], down[:, cols], preferred_element_type=F32
            ).astype(BF)

    def backward_hidden():
        @pl.loop(0, 4)
        def _(r):
            rows = pl.ds(pl.multiple_of(r * 128, 128), 128)
            grad = lax.dot_general(rows_cot[rows, :], down[...], NT, preferred_element_type=F32)
            gate, up = pre[rows, :FF], pre[rows, FF:]
            sigmoid = jax.nn.sigmoid(gate)
            slope = sigmoid * (1.0 + gate * (1.0 - sigmoid))
            slopes[0, rows, :] = (grad * up * slope).astype(BF)
            slopes[1, rows, :] = (grad * (gate * sigmoid)).astype(BF)

    def backward_rows():
        both = jnp.concatenate([slopes[0], slopes[1]], axis=1)

        @pl.loop(0, FULL // 256)
        def _(c):
            cols = pl.ds(pl.multiple_of(c * 256, 256), 256)
            rows_cot[:, cols] = lax.dot_general(both, weights[cols, :], NT, preferred_element_type=F32).astype(BF)

    low = lax.div(here.y * (3 - here.y), 2)
    home_part = lax.div(here.y, 2)
    chunk_of = [lax.rem(here.y + 1, 4), lax.rem(here.y + 3, 4)]
    opposite = lax.rem(here.y + 2, 4)
    away = 1 - here.xh
    step = (1, -1)
    sums = (sum_gate, sum_up)
    ring, plain, mid, mate, cross, twin = {}, {}, {}, {}, {}, {}

    def by_rows(body, height=64):
        @pl.loop(0, FF // height)
        def _(r):
            body(pl.ds(pl.multiple_of(r * height, height), height))

    def part_cols(q):
        return pl.multiple_of((low + q * (3 - 2 * low)) * 1024, 1024)

    def wide(p, q, h):
        return term_wide.at[pl.ds(p * FF, FF), pl.ds(pl.multiple_of(q * 1024 + h * 512, 512), 512)]

    def send_twin_rows():
        chunk = 1 - low + here.core * (1 + 2 * low)
        twin[0] = start(
            remote(
                rows_tok.at[:, pl.ds(pl.multiple_of(chunk * 1024, 1024), 1024)],
                twin_tok.at[:, pl.ds(pl.multiple_of(here.core * 1024, 1024), 1024)],
                twin_send.at[0], twin_recv.at[0], here.twin(),
            )
        )

    def pass_twin_rows():
        twin[0].wait_recv()
        part = twin_tok.at[:, pl.ds(pl.multiple_of(here.core * 1024, 1024), 1024)]
        twin[1] = start(remote(part, part, twin_send.at[1], twin_recv.at[1], here.other_core()))

    def send_twin_slopes():
        for p in range(2):
            twin[2 + p] = start(
                remote(slopes.at[p], twin_slopes.at[p], twin_send.at[2 + p], twin_recv.at[2 + p], here.twin())
            )

    def wide_terms(p, q, small, twin_small):
        @pl.loop(0, 4)
        def _(c):
            cols = pl.ds(pl.multiple_of(part_cols(q) + c * 256, 256), 256)
            at = pl.ds(pl.multiple_of(q * 1024 + c * 256, 256), 256)
            total = jnp.dot(small, rows_tok[:, cols], preferred_element_type=F32)
            total = total + jnp.dot(twin_small, twin_tok[:, at], preferred_element_type=F32)
            term_wide[pl.ds(p * FF, FF), at] = total.astype(BF)

    def send_mate(p):
        for h in range(2):
            mate[p, h] = start(
                remote(wide(p, 1 - home_part, h), got_pair.at[p, h], mate_send.at[p, h], mate_recv.at[p, h], here.mate())
            )

    def cross_wide(p):
        for h in range(2):
            mate[p, h].wait_recv()
        a, b = wide(p, home_part, away), got_pair.at[p, away]

        def body(r):
            a[r, :] = (a[r, :].astype(F32) + b[r, :].astype(F32)).astype(BF)

        by_rows(body)
        cross[p] = start(remote(a, got_wide.at[p], cross_send.at[p], cross_recv.at[p], here.other_xh()))

    def last_wide(p):
        cross[p].wait_recv()
        a, b, c = wide(p, home_part, here.xh), got_pair.at[p, here.xh], got_wide.at[p]
        for n in range(3):
            r = pl.ds(n * 128, 128)
            total = a[r, :].astype(F32) + b[r, :].astype(F32) + c[r, :].astype(F32)
            sums[p][:, r] = total.T.astype(BF)

    def share(chunk, half):
        return term_down.at[:, pl.ds(pl.multiple_of(chunk * 1024 + half * 512, 512), 512)]

    def down_terms(turned, chunk):
        @pl.loop(0, 4)
        def _(c):
            cols = pl.ds(pl.multiple_of(chunk * 1024 + c * 256, 256), 256)
            term_down[:, cols] = jnp.dot(turned, rows_cot[:, cols], preferred_element_type=F32).astype(BF)

    def send_ring():
        for w in range(2):
            ring[w] = start(
                remote(share(opposite, w), first_down.at[w], ring_send.at[w], ring_recv.at[w], here.along_y(step[w]))
            )

    def send_plain():
        for w in range(2):
            plain[w] = start(
                remote(
                    share(chunk_of[w], 1 - w), middle_down.at[w, 1 - w],
                    plain_send.at[w], plain_recv.at[w], here.along_y(step[w]),
                )
            )

    def ring_step():
        for w in range(2):
            ring[w].wait_recv()
            a, b = share(chunk_of[w], w), first_down.at[w]

            def body(r, a=a, b=b):
                a[r, :] = (a[r, :].astype(F32) + b[r, :].astype(F32)).astype(BF)

            by_rows(body)
            mid[w] = start(remote(a, middle_down.at[w, w], mid_send.at[w], mid_recv.at[w], here.along_y(step[w])))

    def cross_down():
        for w in range(2):
            plain[w].wait_recv()
            mid[w].wait_recv()
        a, b, c = share(here.y, away), middle_down.at[0, away], middle_down.at[1, away]

        def body(r):
            a[r, :] = (a[r, :].astype(F32) + b[r, :].astype(F32) + c[r, :].astype(F32)).astype(BF)

        by_rows(body)
        cross[2] = start(remote(a, got_down, cross_send.at[2], cross_recv.at[2], here.other_xh()))

    def last_down():
        cross[2].wait_recv()
        a, b, c = share(here.y, here.xh), middle_down.at[0, here.xh], middle_down.at[1, here.xh]

        def body(r):
            total = a[r, :].astype(F32) + b[r, :].astype(F32) + c[r, :].astype(F32) + got_down[r, :].astype(F32)
            sum_down[r, :] = total.astype(BF)

        by_rows(body)

    parts = (part_out, rows_cot)
    spans = ((10 * CAP, 6 * CAP), (0, 10 * CAP))
    core, side, far, tree = {}, {}, {}, {}

    def swap_halves(a):
        for n, (at, size) in enumerate(spans):
            core[a, n] = start(
                remote(
                    parts[a].at[pl.ds(at, size), theirs], back.at[a, pl.ds(at, size)],
                    core_send.at[a, n], core_recv.at[a, n], here.other_core(),
                )
            )

    def add_halves(a, n):
        core[a, n].wait_recv()
        at, size = spans[n]

        @pl.loop(0, size // CAP)
        def _(r):
            rows = pl.ds(pl.multiple_of(at + r * CAP, CAP), CAP)
            total = parts[a][rows, mine].astype(F32) + back[a, rows, :].astype(F32)
            back[a, rows, :] = total.astype(BF)

    def send_rows(a):
        add_halves(a, 0)
        for w, way in enumerate(step):
            for n in range(3):
                far[a, w, n] = start(
                    remote(
                        back.at[a, pl.ds(FAR[(way, n)] * CAP, CAP)], distant.at[a, w, n],
                        far_send.at[a, w, n], far_recv.at[a, w, n], far_peer(here, way, n, -1),
                    )
                )
        add_halves(a, 1)
        for i in (3, 4, 1, 2, 0):
            side[a, i] = start(
                remote(
                    back.at[a, pl.ds((5 + i) * CAP, CAP)], beside.at[a, i],
                    side_send.at[a, i], side_recv.at[a, i], here.near(1, 0),
                )
            )

    def spread(a, i, more, out):
        side[a, i].wait_recv()
        meta = metas[i]
        slots = slots_of(here, i)
        if a:
            tables = [plain_table(meta, slots).astype(BF)]
        else:
            exact = gate_table(meta, slots)
            high = exact.astype(BF)
            tables = [high, (exact - high.astype(F32)).astype(BF)]

        @pl.loop(0, HALF // COL)
        def _(c):
            cols = pl.ds(pl.multiple_of(c * COL, COL), COL)
            rows = [back[a, pl.ds(i * CAP, CAP), cols], beside[a, i, :, cols]]
            if i >= 3:
                rows += [distant[a, i - 3, n, :, cols] for n in range(3)]
            rows = jnp.concatenate(rows, axis=0)
            total = None
            for table in tables:
                term = lax.dot_general(table, rows, (((0,), (0,)), ((), ())), preferred_element_type=F32)
                total = term if total is None else total + term
            for ref in more:
                total = total + ref[:, cols].astype(F32)
            out[:, cols] = total.astype(BF)

    def sum_two(a):
        for w in range(2):
            for n in range(3):
                far[a, w, n].wait_recv()
            spread(a, 3 + w, [], comp.at[a, w])
            tree[a, w] = start(
                remote(
                    comp.at[a, w], got_two.at[a, w], tree_send.at[a, w], tree_recv.at[a, w], here.near(0, -step[w])
                )
            )

    def sum_one(a):
        for w in range(2):
            tree[a, w].wait_recv()
            spread(a, 1 + w, [got_two.at[a, w]], comp.at[a, 2 + w])
            tree[a, 2 + w] = start(
                remote(
                    comp.at[a, 2 + w], got_one.at[a, w], tree_send.at[a, 2 + w], tree_recv.at[a, 2 + w],
                    here.near(0, -step[w]),
                )
            )

    def sum_home(a, out):
        for w in range(2):
            tree[a, 2 + w].wait_recv()
        spread(a, 0, [got_one.at[a, 0], got_one.at[a, 1]], out)

    first_hop(0)
    for load in loads[1:]:
        load.start()
    metas[0] = make_meta(routes[...], gates[...], dropped[...], placement)
    about = []
    for i in range(1, 5):
        depth, way = STEPS[i]
        about.append(
            start(remote(metas.at[0], metas.at[i], meta_send.at[i - 1], meta_recv.at[i - 1], here.near(0, way * depth)))
        )
    loads[0].wait()
    pick(0, 0)
    second_hop(0)
    for copy in about:
        copy.wait_recv()
    pick(0, 1)
    pick(0, 2)
    loads[1].wait()
    pick(1, 0)
    early = [hop[0, i, 0] for i in (3, 4)]
    for copy in early:
        copy.wait_recv()
    first_hop(1)
    pick(0, 3)
    pick(0, 4)
    second_hop(1)
    pick(1, 1)
    pick(1, 2)
    collect(0)
    send_twin_rows()
    for load in loads[2:]:
        load.wait()
    whole(0)
    forward(0)
    forward(1)
    pick(1, 3)
    pick(1, 4)
    activate()
    forward_out()
    swap_halves(0)
    pass_twin_rows()
    collect(1)
    send_rows(0)
    hidden_turned = hidden[...].T
    whole(1)
    down_terms(hidden_turned, opposite)
    send_ring()
    backward_hidden()
    send_twin_slopes()
    down_terms(hidden_turned, chunk_of[0])
    down_terms(hidden_turned, chunk_of[1])
    send_plain()
    for i in range(1, 5):
        for a in range(2):
            for h in range(2):
                sent(hop[a, i, h])
    sum_two(0)
    ring_step()
    down_terms(hidden_turned, here.y)
    for j in range(16):
        sent(pair[1, j])
    backward_rows()
    swap_halves(1)
    sum_one(0)
    send_rows(1)
    turned = [slopes[p].T for p in range(2)]
    twin[1].wait_recv()
    twin_turned = []
    for p in range(2):
        twin[2 + p].wait_recv()
        twin_turned.append(twin_slopes[p].T)
        wide_terms(p, 1 - home_part, turned[p], twin_turned[p])
        send_mate(p)
    sum_two(1)
    for p in range(2):
        wide_terms(p, home_part, turned[p], twin_turned[p])
    cross_down()
    sum_one(1)
    cross_wide(0)
    sum_home(0, mixed)
    cross_wide(1)
    last_down()
    last_wide(0)
    sum_home(1, input_grad)
    last_wide(1)
    for copy in waiting:
        copy.wait_send()


OUTS = ((TOK, HALF), (TOK, HALF), (512, FF), (512, FF), (FF, 512))


def layer(tok, cot, routes, gates, dropped, placement, w_gate, w_up, w_down):
    vmem = pl.BlockSpec(memory_space=pltpu.VMEM)
    hbm = pl.BlockSpec(memory_space=pl.ANY)
    smem = pl.BlockSpec(memory_space=pltpu.SMEM)
    dma = pltpu.SemaphoreType.DMA
    return pl.pallas_call(
        layer_kernel,
        out_shape=tuple(jax.ShapeDtypeStruct(shape, BF) for shape in OUTS),
        in_specs=[hbm, hbm, vmem, vmem, vmem, smem, hbm, hbm, hbm],
        out_specs=(vmem,) * 5,
        scratch_shapes=[
            pltpu.VMEM((TOK, HALF), BF),
            pltpu.VMEM((TOK, HALF), BF),
            pltpu.VMEM((5, 8, TOK), F32),
            pltpu.VMEM((2, 4, TOK, HALF), BF),
            pltpu.VMEM((2, 11, CAP, HALF), BF),
            pltpu.VMEM((ROWS, FULL), BF),
            pltpu.VMEM((ROWS, FULL), BF),
            pltpu.VMEM((FULL, 2 * FF), BF),
            pltpu.VMEM((FF, FULL), BF),
            pltpu.VMEM((ROWS, 2 * FF), F32),
            pltpu.VMEM((ROWS, FF), BF),
            pltpu.VMEM((2, ROWS, FF), BF),
            pltpu.VMEM((ROWS, FULL), BF),
            pltpu.VMEM((ROWS, HALF), BF),
            pltpu.VMEM((2, ROWS, FF), BF),
            pltpu.VMEM((2 * FF, HALF), BF),
            pltpu.VMEM((FF, FULL), BF),
            pltpu.VMEM((2, ROWS, HALF), BF),
            pltpu.VMEM((2, 5, CAP, HALF), BF),
            pltpu.VMEM((2, 2, 3, CAP, HALF), BF),
            pltpu.VMEM((2, 2, TOK, HALF), BF),
            pltpu.VMEM((2, 2, TOK, HALF), BF),
            pltpu.VMEM((2, 2, FF, 512), BF),
            pltpu.VMEM((2, FF, 512), BF),
            pltpu.VMEM((2, FF, 512), BF),
            pltpu.VMEM((2, 2, FF, 512), BF),
            pltpu.VMEM((FF, 512), BF),
            dma((4,)), dma((4,)),
            dma((2, 4, 2)), dma((2, 4, 2)),
            dma((2, 11)), dma((2, 11)),
            dma((2, 16)), dma((2, 16)),
            dma((2, 2)), dma((2, 2)),
            dma((2, 5)), dma((2, 5)),
            dma((2, 2, 3)), dma((2, 2, 3)),
            dma((2, 4)), dma((2, 4)),
            dma((2,)), dma((2,)),
            dma((2,)), dma((2,)),
            dma((2,)), dma((2,)),
            dma((2, 2)), dma((2, 2)),
            dma((3,)), dma((3,)),
            dma((4,)), dma((4,)),
            dma((5,)),
        ],
        compiler_params=pltpu.CompilerParams(
            collective_id=1, has_side_effects=True, vmem_limit_bytes=63 * MIB
        ),
        name="layer",
    )(tok, cot, routes, gates, dropped, placement, w_gate, w_up, w_down)


def finish_kernel(*refs):
    count = len(OUTS)
    held, load_sem, store_sem = refs[2 * count : 3 * count], refs[3 * count], refs[3 * count + 1]
    loads = [pltpu.make_async_copy(refs[i], held[i], load_sem.at[i]) for i in range(count)]
    stores = [pltpu.make_async_copy(held[i], refs[count + i], store_sem.at[i]) for i in range(count)]
    for load in loads:
        load.start()
    for load, store in zip(loads, stores):
        load.wait()
        store.start()
    for store in stores:
        store.wait()


def finish(*arrays):
    hbm = pl.BlockSpec(memory_space=pl.ANY)
    return pl.pallas_call(
        finish_kernel,
        out_shape=tuple(jax.ShapeDtypeStruct(shape, BF) for shape in OUTS),
        in_specs=[hbm] * len(OUTS),
        out_specs=(hbm,) * len(OUTS),
        scratch_shapes=[pltpu.VMEM(shape, BF) for shape in OUTS]
        + [pltpu.SemaphoreType.DMA((len(OUTS),))] * 2,
        name="finish",
    )(*arrays)


def per_device(tokens, routes, gates, dropped, placement, w_gate, w_up, w_down, cotangent):
    mixed, input_grad, grad_gate, grad_up, grad_down = finish(
        *layer(tokens, cotangent, routes.T, gates.T, dropped.T, placement, w_gate[0], w_up[0], w_down[0])
    )
    return mixed, input_grad, grad_gate[None], grad_up[None], grad_down[None]


def solution(mesh):
    in_specs = (
        P(("dp", "expert"), "tensor"),
        P(("dp", "expert"), None),
        P(("dp", "expert"), None),
        P(("dp", "expert"), None),
        P(),
        P("expert", None, "tensor"),
        P("expert", None, "tensor"),
        P("expert", "tensor", None),
        P(("dp", "expert"), "tensor"),
    )
    out_specs = (
        P(("dp", "expert"), "tensor"),
        P(("dp", "expert"), "tensor"),
        P("expert", "dp", "tensor"),
        P("expert", "dp", "tensor"),
        P("expert", "tensor", "dp"),
    )
    return jax.shard_map(
        per_device, mesh=mesh, in_specs=in_specs, out_specs=out_specs, check_vma=False
    )
```

```python
import jax
import jax.numpy as jnp
from jax import lax
from jax.experimental import pallas as pl
from jax.experimental.pallas import tpu as pltpu
from jax.sharding import PartitionSpec as P

MESH = pl.DeviceIdType.MESH
BF = jnp.bfloat16
F32 = jnp.float32
TOK = 128
CAP = 32
ROWS = 16 * CAP
FULL = 4096
HALF = 2048
FF = 384
COL = 512
MIB = 1 << 20

STEPS = ((0, 0), (1, 1), (1, -1), (2, 1), (2, -1))
FAR = {(1, 0): 10, (1, 1): 11, (-1, 0): 12, (-1, 1): 13, (1, 2): 14, (-1, 2): 15}


class Place:
    def __init__(self):
        self.dp = lax.axis_index("dp")
        expert = lax.axis_index("expert")
        self.core = lax.axis_index("tensor")
        self.y = lax.div(self.dp, 2)
        self.xh = lax.rem(self.dp, 2)
        self.x = lax.div(expert, 8)
        self.z = lax.rem(expert, 8)

    def slot(self, dx, dz):
        return lax.rem(self.x + dx, 2) * 8 + lax.rem(self.z + dz + 8, 8)

    def near(self, dx, dz):
        return (self.dp, self.slot(dx, dz), self.core)

    def other_core(self):
        return (self.dp, self.slot(0, 0), 1 - self.core)

    def along_y(self, dy):
        return (lax.rem(self.y + dy + 4, 4) * 2 + self.xh, self.slot(0, 0), self.core)

    def twin(self):
        y = self.y + 1 - 2 * lax.rem(self.y, 2)
        return (y * 2 + self.xh, self.slot(0, 0), self.core)

    def mate(self):
        return ((3 - self.y) * 2 + self.xh, self.slot(0, 0), self.core)

    def other_xh(self):
        return (self.y * 2 + 1 - self.xh, self.slot(0, 0), self.core)


def barrier(peers):
    sem = pltpu.get_barrier_semaphore()
    for peer in peers:
        pl.semaphore_signal(sem, inc=1, device_id=peer, device_id_type=MESH)
    pl.semaphore_wait(sem, len(peers))


def tree_peers(here):
    return [
        here.near(0, 1), here.near(0, -1), here.near(0, 2), here.near(0, -2), here.near(1, 0),
        here.near(1, 1), here.near(1, -1), here.near(1, 2), here.near(1, -2), here.other_core(),
    ]


def remote(src, dst, send, recv, peer):
    return pltpu.make_async_remote_copy(
        src_ref=src, dst_ref=dst, send_sem=send, recv_sem=recv, device_id=peer, device_id_type=MESH
    )


def slots_of(here, index):
    slots = [here.slot(0, 0), here.slot(1, 0)]
    depth, way = STEPS[index]
    if depth == 2:
        slots += [here.slot(0, way), here.slot(1, way)]
        slots.append(here.slot(0, 2) if way == 1 else here.slot(1, -2))
    return slots


def far_places(index):
    way = STEPS[index][1]
    return [FAR[(way, n)] for n in range(3)]


def far_peer(here, way, n, sign):
    if n == 0:
        return here.near(0, way * sign)
    if n == 1:
        return here.near(1, way * sign)
    return here.near(0, 2 * sign) if way == 1 else here.near(1, -2 * sign)


def hits(meta, slots):
    ids = jnp.concatenate(
        [(s * CAP + lax.broadcasted_iota(jnp.int32, (CAP, TOK), 0)).astype(F32) for s in slots], axis=0
    )
    return meta[0:1, :] == ids, meta[1:2, :] == ids


def plain_table(meta, slots):
    first, second = hits(meta, slots)
    return jnp.where(first | second, 1.0, 0.0).astype(F32)


def gate_table(meta, slots):
    first, second = hits(meta, slots)
    return jnp.where(first, meta[2:3, :], 0.0) + jnp.where(second, meta[3:4, :], 0.0)


def make_meta(routes, gates, dropped, placement):
    row = lax.broadcasted_iota(jnp.int32, (TOK, TOK), 0)
    column = lax.broadcasted_iota(jnp.int32, (TOK, TOK), 1)
    route = [routes[k : k + 1, :] for k in range(2)]
    kept = [dropped[k : k + 1, :] == 0 for k in range(2)]
    gate = [gates[k : k + 1, :] for k in range(2)]
    label = lax.broadcasted_iota(jnp.int32, (16, TOK), 0)
    base = jnp.zeros((16, TOK), F32)
    for e in range(15):
        base = jnp.where(label == e, (placement[e] * CAP).astype(F32), base)
    hit = [jnp.where((route[k] == label) & kept[k], 1.0, 0.0).astype(F32) for k in range(2)]
    before = jnp.dot(
        (hit[0] + hit[1]).astype(BF), jnp.where(row < column, 1.0, 0.0).astype(BF), preferred_element_type=F32
    )
    at = [
        jnp.sum(hit[0] * (before + base), axis=0, keepdims=True),
        jnp.sum(hit[1] * (before + hit[0] + base), axis=0, keepdims=True),
    ]
    out = [jnp.where(kept[k], at[k], -1.0) for k in range(2)]
    out += [jnp.where(kept[k], gate[k], 0.0) for k in range(2)]
    out.append(jnp.zeros((4, TOK), F32))
    return jnp.concatenate(out, axis=0)


NT = (((1,), (1,)), ((), ()))


def layer_kernel(
    tok, cot, routes, gates, dropped, placement, w_gate, w_up, w_down,
    mixed, input_grad, sum_gate, sum_up, sum_down,
    tokv, cotv, metas, comp, sendb, rows_tok, rows_cot, weights, down, pre, hidden, slopes, part_out,
    twin_tok, twin_slopes, term_wide, term_down,
    back, beside, distant, got_two, got_one, got_pair, got_wide, first_down, middle_down, got_down,
    meta_send, meta_recv, hop_send, hop_recv, row_send, row_recv, pair_send, pair_recv,
    core_send, core_recv, side_send, side_recv, far_send, far_recv, tree_send, tree_recv,
    ring_send, ring_recv, plain_send, plain_recv, mid_send, mid_recv, mate_send, mate_recv,
    cross_send, cross_recv, twin_send, twin_recv, load_sem,
):
    here = Place()
    waiting = []

    def start(copy):
        copy.start()
        waiting.append(copy)
        return copy

    def sent(copy):
        waiting[:] = [other for other in waiting if other is not copy]
        copy.wait_send()

    loads = [
        pltpu.make_async_copy(tok, tokv, load_sem.at[0]),
        pltpu.make_async_copy(cot, cotv, load_sem.at[1]),
        pltpu.make_async_copy(w_gate, weights.at[:, pl.ds(0, FF)], load_sem.at[2]),
        pltpu.make_async_copy(w_up, weights.at[:, pl.ds(FF, FF)], load_sem.at[3]),
        pltpu.make_async_copy(w_down, down, load_sem.at[4]),
    ]
    barrier(tree_peers(here) + [here.along_y(1), here.along_y(-1), here.other_xh()])
    loads[0].start()

    source = (tok, cot)
    local = (tokv, cotv)
    final = (rows_tok, rows_cot)
    mine = pl.ds(pl.multiple_of(here.core * HALF, HALF), HALF)
    theirs = pl.ds(pl.multiple_of((1 - here.core) * HALF, HALF), HALF)
    hop, row, pair = {}, {}, {}

    def hop_copy(a, i, h, block):
        cols = pl.ds(h * 1024, 1024)
        way = STEPS[i][1]
        hop[a, i, h] = start(
            remote(
                block.at[:, cols], comp.at[a, i - 1, :, cols],
                hop_send.at[a, i - 1, h], hop_recv.at[a, i - 1, h], here.near(0, way),
            )
        )

    def first_hop(a):
        for h in range(2):
            for i in (1, 2):
                hop_copy(a, i, h, source[a])

    def second_hop(a):
        for h in range(2):
            for i in (1, 2):
                hop[a, i, h].wait_recv()
                hop_copy(a, i + 2, h, comp.at[a, i - 1])

    def to_core(a, j):
        part = final[a].at[pl.ds(j * CAP, CAP), mine]
        pair[a, j] = start(remote(part, part, pair_send.at[a, j], pair_recv.at[a, j], here.other_core()))

    def pick(a, i):
        block = local[a] if i == 0 else comp.at[a, i - 1]
        meta = metas[i]
        slots = slots_of(here, i)
        table = plain_table(meta, slots).astype(BF)
        weight = jnp.sum(gate_table(meta, slots), axis=1, keepdims=True) if a else None
        places = [5 + i] + (far_places(i) if i >= 3 else [])

        def select(c):
            cols = pl.ds(pl.multiple_of(c * COL, COL), COL)
            part = jnp.dot(table, block[:, cols], preferred_element_type=F32)
            if a:
                part = part * weight
            part = part.astype(BF)
            home = pl.ds(pl.multiple_of(here.core * HALF + c * COL, COL), COL)
            final[a][pl.ds(i * CAP, CAP), home] = part[:CAP]
            for n, j in enumerate(places):
                sendb[a, j - 5, :, cols] = part[(n + 1) * CAP : (n + 2) * CAP]

        for h in range(2):
            if i >= 3 and (a or h):
                hop[a, i, h].wait_recv()
            pl.loop(2 * h, 2 * h + 2)(select)
        way = STEPS[i][1]
        for j in places[:0:-1] + places[:1]:
            peer = here.near(1, 0) if j < 10 else far_peer(here, way, places.index(j) - 1, 1)
            row[a, j] = start(
                remote(
                    sendb.at[a, j - 5], final[a].at[pl.ds(j * CAP, CAP), mine],
                    row_send.at[a, j - 5], row_recv.at[a, j - 5], peer,
                )
            )
        to_core(a, i)

    def collect(a):
        for j in range(5, 16):
            row[a, j].wait_recv()
            to_core(a, j)

    def whole(a):
        for j in range(16):
            pair[a, j].wait_recv()

    def forward(r):
        rows = pl.ds(r * 256, 256)

        @pl.loop(0, 3)
        def _(c):
            cols = pl.ds(pl.multiple_of(c * 256, 256), 256)
            pre[rows, cols] = jnp.dot(rows_tok[rows, :], weights[:, cols], preferred_element_type=F32)

    def activate():
        @pl.loop(0, ROWS // 64)
        def _(r):
            rows = pl.ds(pl.multiple_of(r * 64, 64), 64)
            gate = pre[rows, :FF]
            hidden[rows, :] = (gate * jax.nn.sigmoid(gate) * pre[rows, FF:]).astype(BF)

    def forward_out():
        @pl.loop(0, FULL // 256)
        def _(c):
            cols = pl.ds(pl.multiple_of(c * 256, 256), 256)
            part_out[:, cols] = jnp.dot(
                hidden[...], down[:, cols], preferred_element_type=F32
            ).astype(BF)

    def backward_hidden():
        @pl.loop(0, 4)
        def _(r):
            rows = pl.ds(pl.multiple_of(r * 128, 128), 128)
            grad = lax.dot_general(rows_cot[rows, :], down[...], NT, preferred_element_type=F32)
            gate, up = pre[rows, :FF], pre[rows, FF:]
            sigmoid = jax.nn.sigmoid(gate)
            slope = sigmoid * (1.0 + gate * (1.0 - sigmoid))
            slopes[0, rows, :] = (grad * up * slope).astype(BF)
            slopes[1, rows, :] = (grad * (gate * sigmoid)).astype(BF)

    def backward_rows():
        both = jnp.concatenate([slopes[0], slopes[1]], axis=1)

        @pl.loop(0, FULL // 256)
        def _(c):
            cols = pl.ds(pl.multiple_of(c * 256, 256), 256)
            rows_cot[:, cols] = lax.dot_general(both, weights[cols, :], NT, preferred_element_type=F32).astype(BF)

    low = lax.div(here.y * (3 - here.y), 2)
    home_part = lax.div(here.y, 2)
    chunk_of = [lax.rem(here.y + 1, 4), lax.rem(here.y + 3, 4)]
    opposite = lax.rem(here.y + 2, 4)
    away = 1 - here.xh
    step = (1, -1)
    sums = (sum_gate, sum_up)
    ring, plain, mid, mate, cross, twin = {}, {}, {}, {}, {}, {}

    def by_rows(body, height=64):
        @pl.loop(0, FF // height)
        def _(r):
            body(pl.ds(pl.multiple_of(r * height, height), height))

    def part_cols(q):
        return pl.multiple_of((low + q * (3 - 2 * low)) * 1024, 1024)

    def wide(p, q, h):
        return term_wide.at[pl.ds(p * FF, FF), pl.ds(pl.multiple_of(q * 1024 + h * 512, 512), 512)]

    def send_twin_rows():
        chunk = 1 - low + here.core * (1 + 2 * low)
        twin[0] = start(
            remote(
                rows_tok.at[:, pl.ds(pl.multiple_of(chunk * 1024, 1024), 1024)],
                twin_tok.at[:, pl.ds(pl.multiple_of(here.core * 1024, 1024), 1024)],
                twin_send.at[0], twin_recv.at[0], here.twin(),
            )
        )

    def pass_twin_rows():
        twin[0].wait_recv()
        part = twin_tok.at[:, pl.ds(pl.multiple_of(here.core * 1024, 1024), 1024)]
        twin[1] = start(remote(part, part, twin_send.at[1], twin_recv.at[1], here.other_core()))

    def send_twin_slopes():
        for p in range(2):
            twin[2 + p] = start(
                remote(slopes.at[p], twin_slopes.at[p], twin_send.at[2 + p], twin_recv.at[2 + p], here.twin())
            )

    def wide_terms(p, q, small, twin_small):
        @pl.loop(0, 4)
        def _(c):
            cols = pl.ds(pl.multiple_of(part_cols(q) + c * 256, 256), 256)
            at = pl.ds(pl.multiple_of(q * 1024 + c * 256, 256), 256)
            total = jnp.dot(small, rows_tok[:, cols], preferred_element_type=F32)
            total = total + jnp.dot(twin_small, twin_tok[:, at], preferred_element_type=F32)
            term_wide[pl.ds(p * FF, FF), at] = total.astype(BF)

    half_of = (away, here.xh)

    def send_mate(p, n):
        mate[p, n] = start(
            remote(
                wide(p, 1 - home_part, half_of[n]), got_pair.at[p, half_of[n]],
                mate_send.at[p, n], mate_recv.at[p, n], here.mate(),
            )
        )

    def cross_wide(p):
        mate[p, 0].wait_recv()
        a, b = wide(p, home_part, away), got_pair.at[p, away]

        def body(r):
            a[r, :] = (a[r, :].astype(F32) + b[r, :].astype(F32)).astype(BF)

        by_rows(body)
        cross[p] = start(remote(a, got_wide.at[p], cross_send.at[p], cross_recv.at[p], here.other_xh()))

    def last_wide(p):
        mate[p, 1].wait_recv()
        cross[p].wait_recv()
        a, b, c = wide(p, home_part, here.xh), got_pair.at[p, here.xh], got_wide.at[p]
        for n in range(3):
            r = pl.ds(n * 128, 128)
            total = a[r, :].astype(F32) + b[r, :].astype(F32) + c[r, :].astype(F32)
            sums[p][:, r] = total.T.astype(BF)

    def share(chunk, half):
        return term_down.at[:, pl.ds(pl.multiple_of(chunk * 1024 + half * 512, 512), 512)]

    def down_terms(turned, chunk):
        @pl.loop(0, 4)
        def _(c):
            cols = pl.ds(pl.multiple_of(chunk * 1024 + c * 256, 256), 256)
            term_down[:, cols] = jnp.dot(turned, rows_cot[:, cols], preferred_element_type=F32).astype(BF)

    def send_ring():
        for w in range(2):
            ring[w] = start(
                remote(share(opposite, w), first_down.at[w], ring_send.at[w], ring_recv.at[w], here.along_y(step[w]))
            )

    def send_plain():
        for w in range(2):
            plain[w] = start(
                remote(
                    share(chunk_of[w], 1 - w), middle_down.at[w, 1 - w],
                    plain_send.at[w], plain_recv.at[w], here.along_y(step[w]),
                )
            )

    def ring_step():
        for w in range(2):
            ring[w].wait_recv()
            a, b = share(chunk_of[w], w), first_down.at[w]

            def body(r, a=a, b=b):
                a[r, :] = (a[r, :].astype(F32) + b[r, :].astype(F32)).astype(BF)

            by_rows(body)
            mid[w] = start(remote(a, middle_down.at[w, w], mid_send.at[w], mid_recv.at[w], here.along_y(step[w])))

    def cross_down():
        for w in range(2):
            plain[w].wait_recv()
            mid[w].wait_recv()
        a, b, c = share(here.y, away), middle_down.at[0, away], middle_down.at[1, away]

        def body(r):
            a[r, :] = (a[r, :].astype(F32) + b[r, :].astype(F32) + c[r, :].astype(F32)).astype(BF)

        by_rows(body)
        cross[2] = start(remote(a, got_down, cross_send.at[2], cross_recv.at[2], here.other_xh()))

    def last_down():
        cross[2].wait_recv()
        a, b, c = share(here.y, here.xh), middle_down.at[0, here.xh], middle_down.at[1, here.xh]

        def body(r):
            total = a[r, :].astype(F32) + b[r, :].astype(F32) + c[r, :].astype(F32) + got_down[r, :].astype(F32)
            sum_down[r, :] = total.astype(BF)

        by_rows(body)

    parts = (part_out, rows_cot)
    spans = ((10 * CAP, 6 * CAP), (0, 10 * CAP))
    core, side, far, tree = {}, {}, {}, {}

    def swap_halves(a):
        for n, (at, size) in enumerate(spans):
            core[a, n] = start(
                remote(
                    parts[a].at[pl.ds(at, size), theirs], back.at[a, pl.ds(at, size)],
                    core_send.at[a, n], core_recv.at[a, n], here.other_core(),
                )
            )

    def add_halves(a, n):
        core[a, n].wait_recv()
        at, size = spans[n]

        @pl.loop(0, size // CAP)
        def _(r):
            rows = pl.ds(pl.multiple_of(at + r * CAP, CAP), CAP)
            total = parts[a][rows, mine].astype(F32) + back[a, rows, :].astype(F32)
            back[a, rows, :] = total.astype(BF)

    def send_rows(a):
        add_halves(a, 0)
        for w, way in enumerate(step):
            for n in range(3):
                far[a, w, n] = start(
                    remote(
                        back.at[a, pl.ds(FAR[(way, n)] * CAP, CAP)], distant.at[a, w, n],
                        far_send.at[a, w, n], far_recv.at[a, w, n], far_peer(here, way, n, -1),
                    )
                )
        add_halves(a, 1)
        for i in (3, 4, 1, 2, 0):
            side[a, i] = start(
                remote(
                    back.at[a, pl.ds((5 + i) * CAP, CAP)], beside.at[a, i],
                    side_send.at[a, i], side_recv.at[a, i], here.near(1, 0),
                )
            )

    def spread(a, i, more, out):
        side[a, i].wait_recv()
        meta = metas[i]
        slots = slots_of(here, i)
        if a:
            tables = [plain_table(meta, slots).astype(BF)]
        else:
            exact = gate_table(meta, slots)
            high = exact.astype(BF)
            tables = [high, (exact - high.astype(F32)).astype(BF)]

        @pl.loop(0, HALF // COL)
        def _(c):
            cols = pl.ds(pl.multiple_of(c * COL, COL), COL)
            rows = [back[a, pl.ds(i * CAP, CAP), cols], beside[a, i, :, cols]]
            if i >= 3:
                rows += [distant[a, i - 3, n, :, cols] for n in range(3)]
            rows = jnp.concatenate(rows, axis=0)
            total = None
            for table in tables:
                term = lax.dot_general(table, rows, (((0,), (0,)), ((), ())), preferred_element_type=F32)
                total = term if total is None else total + term
            for ref in more:
                total = total + ref[:, cols].astype(F32)
            out[:, cols] = total.astype(BF)

    def sum_two(a):
        for w in range(2):
            for n in range(3):
                far[a, w, n].wait_recv()
            spread(a, 3 + w, [], comp.at[a, w])
            tree[a, w] = start(
                remote(
                    comp.at[a, w], got_two.at[a, w], tree_send.at[a, w], tree_recv.at[a, w], here.near(0, -step[w])
                )
            )

    def sum_one(a):
        for w in range(2):
            tree[a, w].wait_recv()
            spread(a, 1 + w, [got_two.at[a, w]], comp.at[a, 2 + w])
            tree[a, 2 + w] = start(
                remote(
                    comp.at[a, 2 + w], got_one.at[a, w], tree_send.at[a, 2 + w], tree_recv.at[a, 2 + w],
                    here.near(0, -step[w]),
                )
            )

    def sum_home(a, out):
        for w in range(2):
            tree[a, 2 + w].wait_recv()
        spread(a, 0, [got_one.at[a, 0], got_one.at[a, 1]], out)

    first_hop(0)
    for load in loads[1:]:
        load.start()
    metas[0] = make_meta(routes[...], gates[...], dropped[...], placement)
    about = []
    for i in range(1, 5):
        depth, way = STEPS[i]
        about.append(
            start(remote(metas.at[0], metas.at[i], meta_send.at[i - 1], meta_recv.at[i - 1], here.near(0, way * depth)))
        )
    loads[0].wait()
    pick(0, 0)
    second_hop(0)
    for copy in about:
        copy.wait_recv()
    pick(0, 1)
    pick(0, 2)
    loads[1].wait()
    pick(1, 0)
    early = [hop[0, i, 0] for i in (3, 4)]
    for copy in early:
        copy.wait_recv()
    first_hop(1)
    pick(0, 3)
    pick(0, 4)
    second_hop(1)
    pick(1, 1)
    pick(1, 2)
    collect(0)
    send_twin_rows()
    for load in loads[2:]:
        load.wait()
    whole(0)
    forward(0)
    forward(1)
    pick(1, 3)
    pick(1, 4)
    activate()
    forward_out()
    swap_halves(0)
    collect(1)
    send_rows(0)
    hidden_turned = hidden[...].T
    whole(1)
    down_terms(hidden_turned, opposite)
    send_ring()
    backward_hidden()
    send_twin_slopes()
    pass_twin_rows()
    down_terms(hidden_turned, chunk_of[0])
    down_terms(hidden_turned, chunk_of[1])
    send_plain()
    for i in range(1, 5):
        for a in range(2):
            for h in range(2):
                sent(hop[a, i, h])
    sum_two(0)
    ring_step()
    down_terms(hidden_turned, here.y)
    for j in range(16):
        sent(pair[1, j])
    backward_rows()
    swap_halves(1)
    sum_one(0)
    send_rows(1)
    turned = [slopes[p].T for p in range(2)]
    twin[1].wait_recv()
    twin_turned = []
    for p in range(2):
        twin[2 + p].wait_recv()
        twin_turned.append(twin_slopes[p].T)
        wide_terms(p, 1 - home_part, turned[p], twin_turned[p])
        send_mate(p, 0)
    for p in range(2):
        send_mate(p, 1)
    for p in range(2):
        wide_terms(p, home_part, turned[p], twin_turned[p])
    sum_two(1)
    cross_wide(0)
    cross_wide(1)
    sum_home(0, mixed)
    sum_one(1)
    cross_down()
    last_down()
    last_wide(0)
    last_wide(1)
    sum_home(1, input_grad)
    for copy in waiting:
        copy.wait_send()


OUTS = ((TOK, HALF), (TOK, HALF), (512, FF), (512, FF), (FF, 512))


def layer(tok, cot, routes, gates, dropped, placement, w_gate, w_up, w_down):
    vmem = pl.BlockSpec(memory_space=pltpu.VMEM)
    hbm = pl.BlockSpec(memory_space=pl.ANY)
    smem = pl.BlockSpec(memory_space=pltpu.SMEM)
    dma = pltpu.SemaphoreType.DMA
    return pl.pallas_call(
        layer_kernel,
        out_shape=tuple(jax.ShapeDtypeStruct(shape, BF) for shape in OUTS),
        in_specs=[hbm, hbm, vmem, vmem, vmem, smem, hbm, hbm, hbm],
        out_specs=(vmem,) * 5,
        scratch_shapes=[
            pltpu.VMEM((TOK, HALF), BF),
            pltpu.VMEM((TOK, HALF), BF),
            pltpu.VMEM((5, 8, TOK), F32),
            pltpu.VMEM((2, 4, TOK, HALF), BF),
            pltpu.VMEM((2, 11, CAP, HALF), BF),
            pltpu.VMEM((ROWS, FULL), BF),
            pltpu.VMEM((ROWS, FULL), BF),
            pltpu.VMEM((FULL, 2 * FF), BF),
            pltpu.VMEM((FF, FULL), BF),
            pltpu.VMEM((ROWS, 2 * FF), F32),
            pltpu.VMEM((ROWS, FF), BF),
            pltpu.VMEM((2, ROWS, FF), BF),
            pltpu.VMEM((ROWS, FULL), BF),
            pltpu.VMEM((ROWS, HALF), BF),
            pltpu.VMEM((2, ROWS, FF), BF),
            pltpu.VMEM((2 * FF, HALF), BF),
            pltpu.VMEM((FF, FULL), BF),
            pltpu.VMEM((2, ROWS, HALF), BF),
            pltpu.VMEM((2, 5, CAP, HALF), BF),
            pltpu.VMEM((2, 2, 3, CAP, HALF), BF),
            pltpu.VMEM((2, 2, TOK, HALF), BF),
            pltpu.VMEM((2, 2, TOK, HALF), BF),
            pltpu.VMEM((2, 2, FF, 512), BF),
            pltpu.VMEM((2, FF, 512), BF),
            pltpu.VMEM((2, FF, 512), BF),
            pltpu.VMEM((2, 2, FF, 512), BF),
            pltpu.VMEM((FF, 512), BF),
            dma((4,)), dma((4,)),
            dma((2, 4, 2)), dma((2, 4, 2)),
            dma((2, 11)), dma((2, 11)),
            dma((2, 16)), dma((2, 16)),
            dma((2, 2)), dma((2, 2)),
            dma((2, 5)), dma((2, 5)),
            dma((2, 2, 3)), dma((2, 2, 3)),
            dma((2, 4)), dma((2, 4)),
            dma((2,)), dma((2,)),
            dma((2,)), dma((2,)),
            dma((2,)), dma((2,)),
            dma((2, 2)), dma((2, 2)),
            dma((3,)), dma((3,)),
            dma((4,)), dma((4,)),
            dma((5,)),
        ],
        compiler_params=pltpu.CompilerParams(
            collective_id=1, has_side_effects=True, vmem_limit_bytes=63 * MIB
        ),
        name="layer",
    )(tok, cot, routes, gates, dropped, placement, w_gate, w_up, w_down)


def finish_kernel(*refs):
    count = len(OUTS)
    held, load_sem, store_sem = refs[2 * count : 3 * count], refs[3 * count], refs[3 * count + 1]
    loads = [pltpu.make_async_copy(refs[i], held[i], load_sem.at[i]) for i in range(count)]
    stores = [pltpu.make_async_copy(held[i], refs[count + i], store_sem.at[i]) for i in range(count)]
    for load in loads:
        load.start()
    for load, store in zip(loads, stores):
        load.wait()
        store.start()
    for store in stores:
        store.wait()


def finish(*arrays):
    hbm = pl.BlockSpec(memory_space=pl.ANY)
    return pl.pallas_call(
        finish_kernel,
        out_shape=tuple(jax.ShapeDtypeStruct(shape, BF) for shape in OUTS),
        in_specs=[hbm] * len(OUTS),
        out_specs=(hbm,) * len(OUTS),
        scratch_shapes=[pltpu.VMEM(shape, BF) for shape in OUTS]
        + [pltpu.SemaphoreType.DMA((len(OUTS),))] * 2,
        name="finish",
    )(*arrays)


def per_device(tokens, routes, gates, dropped, placement, w_gate, w_up, w_down, cotangent):
    mixed, input_grad, grad_gate, grad_up, grad_down = finish(
        *layer(tokens, cotangent, routes.T, gates.T, dropped.T, placement, w_gate[0], w_up[0], w_down[0])
    )
    return mixed, input_grad, grad_gate[None], grad_up[None], grad_down[None]


def solution(mesh):
    in_specs = (
        P(("dp", "expert"), "tensor"),
        P(("dp", "expert"), None),
        P(("dp", "expert"), None),
        P(("dp", "expert"), None),
        P(),
        P("expert", None, "tensor"),
        P("expert", None, "tensor"),
        P("expert", "tensor", None),
        P(("dp", "expert"), "tensor"),
    )
    out_specs = (
        P(("dp", "expert"), "tensor"),
        P(("dp", "expert"), "tensor"),
        P("expert", "dp", "tensor"),
        P("expert", "dp", "tensor"),
        P("expert", "tensor", "dp"),
    )
    return jax.shard_map(
        per_device, mesh=mesh, in_specs=in_specs, out_specs=out_specs, check_vma=False
    )
```

```python
import jax
import jax.numpy as jnp
from jax import lax
from jax.experimental import pallas as pl
from jax.experimental.pallas import tpu as pltpu
from jax.sharding import PartitionSpec as P

MESH = pl.DeviceIdType.MESH
BF = jnp.bfloat16
F32 = jnp.float32
TOK = 128
CAP = 32
ROWS = 16 * CAP
FULL = 4096
HALF = 2048
FF = 384
COL = 512
MIB = 1 << 20

STEPS = ((0, 0), (1, 1), (1, -1), (2, 1), (2, -1))
FAR = {(1, 0): 10, (1, 1): 11, (-1, 0): 12, (-1, 1): 13, (1, 2): 14, (-1, 2): 15}


class Place:
    def __init__(self):
        self.dp = lax.axis_index("dp")
        expert = lax.axis_index("expert")
        self.core = lax.axis_index("tensor")
        self.y = lax.div(self.dp, 2)
        self.xh = lax.rem(self.dp, 2)
        self.x = lax.div(expert, 8)
        self.z = lax.rem(expert, 8)

    def slot(self, dx, dz):
        return lax.rem(self.x + dx, 2) * 8 + lax.rem(self.z + dz + 8, 8)

    def near(self, dx, dz):
        return (self.dp, self.slot(dx, dz), self.core)

    def other_core(self):
        return (self.dp, self.slot(0, 0), 1 - self.core)

    def along_y(self, dy):
        return (lax.rem(self.y + dy + 4, 4) * 2 + self.xh, self.slot(0, 0), self.core)

    def twin(self):
        y = self.y + 1 - 2 * lax.rem(self.y, 2)
        return (y * 2 + self.xh, self.slot(0, 0), self.core)

    def mate(self):
        return ((3 - self.y) * 2 + self.xh, self.slot(0, 0), self.core)

    def other_xh(self):
        return (self.y * 2 + 1 - self.xh, self.slot(0, 0), self.core)


def barrier(peers, meanwhile):
    sem = pltpu.get_barrier_semaphore()
    for peer in peers:
        pl.semaphore_signal(sem, inc=1, device_id=peer, device_id_type=MESH)
    meanwhile()
    pl.semaphore_wait(sem, len(peers))


def tree_peers(here):
    return [
        here.near(0, 1), here.near(0, -1), here.near(0, 2), here.near(0, -2), here.near(1, 0),
        here.near(1, 1), here.near(1, -1), here.near(1, 2), here.near(1, -2), here.other_core(),
    ]


def remote(src, dst, send, recv, peer):
    return pltpu.make_async_remote_copy(
        src_ref=src, dst_ref=dst, send_sem=send, recv_sem=recv, device_id=peer, device_id_type=MESH
    )


def slots_of(here, index):
    slots = [here.slot(0, 0), here.slot(1, 0)]
    depth, way = STEPS[index]
    if depth == 2:
        slots += [here.slot(0, way), here.slot(1, way)]
        slots.append(here.slot(0, 2) if way == 1 else here.slot(1, -2))
    return slots


def far_places(index):
    way = STEPS[index][1]
    return [FAR[(way, n)] for n in range(3)]


def far_peer(here, way, n, sign):
    if n == 0:
        return here.near(0, way * sign)
    if n == 1:
        return here.near(1, way * sign)
    return here.near(0, 2 * sign) if way == 1 else here.near(1, -2 * sign)


def hits(meta, slots):
    ids = jnp.concatenate(
        [(s * CAP + lax.broadcasted_iota(jnp.int32, (CAP, TOK), 0)).astype(F32) for s in slots], axis=0
    )
    return meta[0:1, :] == ids, meta[1:2, :] == ids


def plain_table(meta, slots):
    first, second = hits(meta, slots)
    return jnp.where(first | second, 1.0, 0.0).astype(F32)


def gate_table(meta, slots):
    first, second = hits(meta, slots)
    return jnp.where(first, meta[2:3, :], 0.0) + jnp.where(second, meta[3:4, :], 0.0)


def make_meta(routes, gates, dropped, placement):
    row = lax.broadcasted_iota(jnp.int32, (TOK, TOK), 0)
    column = lax.broadcasted_iota(jnp.int32, (TOK, TOK), 1)
    route = [routes[k : k + 1, :] for k in range(2)]
    kept = [dropped[k : k + 1, :] == 0 for k in range(2)]
    gate = [gates[k : k + 1, :] for k in range(2)]
    label = lax.broadcasted_iota(jnp.int32, (16, TOK), 0)
    base = jnp.zeros((16, TOK), F32)
    for e in range(15):
        base = jnp.where(label == e, (placement[e] * CAP).astype(F32), base)
    hit = [jnp.where((route[k] == label) & kept[k], 1.0, 0.0).astype(F32) for k in range(2)]
    before = jnp.dot(
        (hit[0] + hit[1]).astype(BF), jnp.where(row < column, 1.0, 0.0).astype(BF), preferred_element_type=F32
    )
    at = [
        jnp.sum(hit[0] * (before + base), axis=0, keepdims=True),
        jnp.sum(hit[1] * (before + hit[0] + base), axis=0, keepdims=True),
    ]
    out = [jnp.where(kept[k], at[k], -1.0) for k in range(2)]
    out += [jnp.where(kept[k], gate[k], 0.0) for k in range(2)]
    out.append(jnp.zeros((4, TOK), F32))
    return jnp.concatenate(out, axis=0)


NT = (((1,), (1,)), ((), ()))


def layer_kernel(
    tok, cot, routes, gates, dropped, placement, w_gate, w_up, w_down,
    mixed, input_grad, sum_gate, sum_up, sum_down,
    tokv, cotv, metas, comp, sendb, rows_tok, rows_cot, weights, down, pre, hidden, slopes, part_out,
    twin_tok, twin_slopes, term_wide, term_down,
    back, beside, distant, got_two, got_one, got_pair, got_wide, first_down, middle_down, got_down,
    meta_send, meta_recv, hop_send, hop_recv, row_send, row_recv, pair_send, pair_recv,
    core_send, core_recv, side_send, side_recv, far_send, far_recv, tree_send, tree_recv,
    ring_send, ring_recv, plain_send, plain_recv, mid_send, mid_recv, mate_send, mate_recv,
    cross_send, cross_recv, twin_send, twin_recv, load_sem,
):
    here = Place()
    waiting = []

    def start(copy):
        copy.start()
        waiting.append(copy)
        return copy

    def sent(copy):
        waiting[:] = [other for other in waiting if other is not copy]
        copy.wait_send()

    loads = [
        pltpu.make_async_copy(tok, tokv, load_sem.at[0]),
        pltpu.make_async_copy(cot, cotv, load_sem.at[1]),
        pltpu.make_async_copy(w_gate, weights.at[:, pl.ds(0, FF)], load_sem.at[2]),
        pltpu.make_async_copy(w_up, weights.at[:, pl.ds(FF, FF)], load_sem.at[3]),
        pltpu.make_async_copy(w_down, down, load_sem.at[4]),
    ]

    def prepare():
        for load in loads:
            load.start()
        metas[0] = make_meta(routes[...], gates[...], dropped[...], placement)

    barrier(tree_peers(here) + [here.along_y(1), here.along_y(-1), here.other_xh()], prepare)

    source = (tok, cot)
    local = (tokv, cotv)
    final = (rows_tok, rows_cot)
    mine = pl.ds(pl.multiple_of(here.core * HALF, HALF), HALF)
    theirs = pl.ds(pl.multiple_of((1 - here.core) * HALF, HALF), HALF)
    hop, row, pair = {}, {}, {}

    def hop_copy(a, i, h, block):
        cols = pl.ds(h * 1024, 1024)
        way = STEPS[i][1]
        hop[a, i, h] = start(
            remote(
                block.at[:, cols], comp.at[a, i - 1, :, cols],
                hop_send.at[a, i - 1, h], hop_recv.at[a, i - 1, h], here.near(0, way),
            )
        )

    def first_hop(a):
        for h in range(2):
            for i in (1, 2):
                hop_copy(a, i, h, source[a])

    def second_hop(a):
        for h in range(2):
            for i in (1, 2):
                hop[a, i, h].wait_recv()
                hop_copy(a, i + 2, h, comp.at[a, i - 1])

    def to_core(a, j):
        part = final[a].at[pl.ds(j * CAP, CAP), mine]
        pair[a, j] = start(remote(part, part, pair_send.at[a, j], pair_recv.at[a, j], here.other_core()))

    def pick(a, i):
        block = local[a] if i == 0 else comp.at[a, i - 1]
        meta = metas[i]
        slots = slots_of(here, i)
        table = plain_table(meta, slots).astype(BF)
        weight = jnp.sum(gate_table(meta, slots), axis=1, keepdims=True) if a else None
        places = [5 + i] + (far_places(i) if i >= 3 else [])

        def select(c):
            cols = pl.ds(pl.multiple_of(c * COL, COL), COL)
            part = jnp.dot(table, block[:, cols], preferred_element_type=F32)
            if a:
                part = part * weight
            part = part.astype(BF)
            home = pl.ds(pl.multiple_of(here.core * HALF + c * COL, COL), COL)
            final[a][pl.ds(i * CAP, CAP), home] = part[:CAP]
            for n, j in enumerate(places):
                sendb[a, j - 5, :, cols] = part[(n + 1) * CAP : (n + 2) * CAP]

        for h in range(2):
            if i >= 3 and (a or h):
                hop[a, i, h].wait_recv()
            pl.loop(2 * h, 2 * h + 2)(select)
        way = STEPS[i][1]
        for j in places[:0:-1] + places[:1]:
            peer = here.near(1, 0) if j < 10 else far_peer(here, way, places.index(j) - 1, 1)
            row[a, j] = start(
                remote(
                    sendb.at[a, j - 5], final[a].at[pl.ds(j * CAP, CAP), mine],
                    row_send.at[a, j - 5], row_recv.at[a, j - 5], peer,
                )
            )
        to_core(a, i)

    def collect(a):
        for j in range(5, 16):
            row[a, j].wait_recv()
            to_core(a, j)

    def whole(a):
        for j in range(16):
            pair[a, j].wait_recv()

    def forward(r):
        rows = pl.ds(r * 256, 256)

        @pl.loop(0, 3)
        def _(c):
            cols = pl.ds(pl.multiple_of(c * 256, 256), 256)
            pre[rows, cols] = jnp.dot(rows_tok[rows, :], weights[:, cols], preferred_element_type=F32)

    def activate():
        @pl.loop(0, ROWS // 64)
        def _(r):
            rows = pl.ds(pl.multiple_of(r * 64, 64), 64)
            gate = pre[rows, :FF]
            hidden[rows, :] = (gate * jax.nn.sigmoid(gate) * pre[rows, FF:]).astype(BF)

    def forward_out():
        @pl.loop(0, FULL // 256)
        def _(c):
            cols = pl.ds(pl.multiple_of(c * 256, 256), 256)
            part_out[:, cols] = jnp.dot(
                hidden[...], down[:, cols], preferred_element_type=F32
            ).astype(BF)

    def backward_hidden():
        @pl.loop(0, 4)
        def _(r):
            rows = pl.ds(pl.multiple_of(r * 128, 128), 128)
            grad = lax.dot_general(rows_cot[rows, :], down[...], NT, preferred_element_type=F32)
            gate, up = pre[rows, :FF], pre[rows, FF:]
            sigmoid = jax.nn.sigmoid(gate)
            slope = sigmoid * (1.0 + gate * (1.0 - sigmoid))
            slopes[0, rows, :] = (grad * up * slope).astype(BF)
            slopes[1, rows, :] = (grad * (gate * sigmoid)).astype(BF)

    def backward_rows():
        both = jnp.concatenate([slopes[0], slopes[1]], axis=1)

        @pl.loop(0, FULL // 256)
        def _(c):
            cols = pl.ds(pl.multiple_of(c * 256, 256), 256)
            rows_cot[:, cols] = lax.dot_general(both, weights[cols, :], NT, preferred_element_type=F32).astype(BF)

    low = lax.div(here.y * (3 - here.y), 2)
    home_part = lax.div(here.y, 2)
    chunk_of = [lax.rem(here.y + 1, 4), lax.rem(here.y + 3, 4)]
    opposite = lax.rem(here.y + 2, 4)
    away = 1 - here.xh
    step = (1, -1)
    sums = (sum_gate, sum_up)
    ring, plain, mid, mate, cross, twin = {}, {}, {}, {}, {}, {}

    def by_rows(body, height=64):
        @pl.loop(0, FF // height)
        def _(r):
            body(pl.ds(pl.multiple_of(r * height, height), height))

    def part_cols(q):
        return pl.multiple_of((low + q * (3 - 2 * low)) * 1024, 1024)

    def wide(p, q, h):
        return term_wide.at[pl.ds(p * FF, FF), pl.ds(pl.multiple_of(q * 1024 + h * 512, 512), 512)]

    def send_twin_rows():
        chunk = 1 - low + here.core * (1 + 2 * low)
        twin[0] = start(
            remote(
                rows_tok.at[:, pl.ds(pl.multiple_of(chunk * 1024, 1024), 1024)],
                twin_tok.at[:, pl.ds(pl.multiple_of(here.core * 1024, 1024), 1024)],
                twin_send.at[0], twin_recv.at[0], here.twin(),
            )
        )

    def pass_twin_rows():
        twin[0].wait_recv()
        part = twin_tok.at[:, pl.ds(pl.multiple_of(here.core * 1024, 1024), 1024)]
        twin[1] = start(remote(part, part, twin_send.at[1], twin_recv.at[1], here.other_core()))

    def send_twin_slopes():
        for p in range(2):
            twin[2 + p] = start(
                remote(slopes.at[p], twin_slopes.at[p], twin_send.at[2 + p], twin_recv.at[2 + p], here.twin())
            )

    def wide_terms(p, q, small, twin_small):
        @pl.loop(0, 4)
        def _(c):
            cols = pl.ds(pl.multiple_of(part_cols(q) + c * 256, 256), 256)
            at = pl.ds(pl.multiple_of(q * 1024 + c * 256, 256), 256)
            total = jnp.dot(small, rows_tok[:, cols], preferred_element_type=F32)
            total = total + jnp.dot(twin_small, twin_tok[:, at], preferred_element_type=F32)
            term_wide[pl.ds(p * FF, FF), at] = total.astype(BF)

    half_of = (away, here.xh)

    def send_mate(p, n):
        mate[p, n] = start(
            remote(
                wide(p, 1 - home_part, half_of[n]), got_pair.at[p, half_of[n]],
                mate_send.at[p, n], mate_recv.at[p, n], here.mate(),
            )
        )

    def cross_wide(p):
        mate[p, 0].wait_recv()
        a, b = wide(p, home_part, away), got_pair.at[p, away]

        def body(r):
            a[r, :] = (a[r, :].astype(F32) + b[r, :].astype(F32)).astype(BF)

        by_rows(body)
        cross[p] = start(remote(a, got_wide.at[p], cross_send.at[p], cross_recv.at[p], here.other_xh()))

    def last_wide(p):
        mate[p, 1].wait_recv()
        cross[p].wait_recv()
        a, b, c = wide(p, home_part, here.xh), got_pair.at[p, here.xh], got_wide.at[p]
        for n in range(3):
            r = pl.ds(n * 128, 128)
            total = a[r, :].astype(F32) + b[r, :].astype(F32) + c[r, :].astype(F32)
            sums[p][:, r] = total.T.astype(BF)

    def share(chunk, half):
        return term_down.at[:, pl.ds(pl.multiple_of(chunk * 1024 + half * 512, 512), 512)]

    def down_terms(turned, chunk):
        @pl.loop(0, 4)
        def _(c):
            cols = pl.ds(pl.multiple_of(chunk * 1024 + c * 256, 256), 256)
            term_down[:, cols] = jnp.dot(turned, rows_cot[:, cols], preferred_element_type=F32).astype(BF)

    def send_ring():
        for w in range(2):
            ring[w] = start(
                remote(share(opposite, w), first_down.at[w], ring_send.at[w], ring_recv.at[w], here.along_y(step[w]))
            )

    def send_plain():
        for w in range(2):
            plain[w] = start(
                remote(
                    share(chunk_of[w], 1 - w), middle_down.at[w, 1 - w],
                    plain_send.at[w], plain_recv.at[w], here.along_y(step[w]),
                )
            )

    def ring_step():
        for w in range(2):
            ring[w].wait_recv()
            a, b = share(chunk_of[w], w), first_down.at[w]

            def body(r, a=a, b=b):
                a[r, :] = (a[r, :].astype(F32) + b[r, :].astype(F32)).astype(BF)

            by_rows(body)
            mid[w] = start(remote(a, middle_down.at[w, w], mid_send.at[w], mid_recv.at[w], here.along_y(step[w])))

    def cross_down():
        for w in range(2):
            plain[w].wait_recv()
            mid[w].wait_recv()
        a, b, c = share(here.y, away), middle_down.at[0, away], middle_down.at[1, away]

        def body(r):
            a[r, :] = (a[r, :].astype(F32) + b[r, :].astype(F32) + c[r, :].astype(F32)).astype(BF)

        by_rows(body)
        cross[2] = start(remote(a, got_down, cross_send.at[2], cross_recv.at[2], here.other_xh()))

    def last_down():
        cross[2].wait_recv()
        a, b, c = share(here.y, here.xh), middle_down.at[0, here.xh], middle_down.at[1, here.xh]

        def body(r):
            total = a[r, :].astype(F32) + b[r, :].astype(F32) + c[r, :].astype(F32) + got_down[r, :].astype(F32)
            sum_down[r, :] = total.astype(BF)

        by_rows(body)

    parts = (part_out, rows_cot)
    spans = ((10 * CAP, 6 * CAP), (0, 10 * CAP))
    core, side, far, tree = {}, {}, {}, {}

    def swap_halves(a):
        for n, (at, size) in enumerate(spans):
            core[a, n] = start(
                remote(
                    parts[a].at[pl.ds(at, size), theirs], back.at[a, pl.ds(at, size)],
                    core_send.at[a, n], core_recv.at[a, n], here.other_core(),
                )
            )

    def add_halves(a, n):
        core[a, n].wait_recv()
        at, size = spans[n]

        @pl.loop(0, size // CAP)
        def _(r):
            rows = pl.ds(pl.multiple_of(at + r * CAP, CAP), CAP)
            total = parts[a][rows, mine].astype(F32) + back[a, rows, :].astype(F32)
            back[a, rows, :] = total.astype(BF)

    def send_rows(a):
        add_halves(a, 0)
        for w, way in enumerate(step):
            for n in range(3):
                far[a, w, n] = start(
                    remote(
                        back.at[a, pl.ds(FAR[(way, n)] * CAP, CAP)], distant.at[a, w, n],
                        far_send.at[a, w, n], far_recv.at[a, w, n], far_peer(here, way, n, -1),
                    )
                )
        add_halves(a, 1)
        for i in (3, 4, 1, 2, 0):
            side[a, i] = start(
                remote(
                    back.at[a, pl.ds((5 + i) * CAP, CAP)], beside.at[a, i],
                    side_send.at[a, i], side_recv.at[a, i], here.near(1, 0),
                )
            )

    def spread(a, i, more, out):
        side[a, i].wait_recv()
        meta = metas[i]
        slots = slots_of(here, i)
        if a:
            tables = [plain_table(meta, slots).astype(BF)]
        else:
            exact = gate_table(meta, slots)
            high = exact.astype(BF)
            tables = [high, (exact - high.astype(F32)).astype(BF)]

        @pl.loop(0, HALF // COL)
        def _(c):
            cols = pl.ds(pl.multiple_of(c * COL, COL), COL)
            rows = [back[a, pl.ds(i * CAP, CAP), cols], beside[a, i, :, cols]]
            if i >= 3:
                rows += [distant[a, i - 3, n, :, cols] for n in range(3)]
            rows = jnp.concatenate(rows, axis=0)
            total = None
            for table in tables:
                term = lax.dot_general(table, rows, (((0,), (0,)), ((), ())), preferred_element_type=F32)
                total = term if total is None else total + term
            for ref in more:
                total = total + ref[:, cols].astype(F32)
            out[:, cols] = total.astype(BF)

    def sum_two(a):
        for w in range(2):
            for n in range(3):
                far[a, w, n].wait_recv()
            spread(a, 3 + w, [], comp.at[a, w])
            tree[a, w] = start(
                remote(
                    comp.at[a, w], got_two.at[a, w], tree_send.at[a, w], tree_recv.at[a, w], here.near(0, -step[w])
                )
            )

    def sum_one(a):
        for w in range(2):
            tree[a, w].wait_recv()
            spread(a, 1 + w, [got_two.at[a, w]], comp.at[a, 2 + w])
            tree[a, 2 + w] = start(
                remote(
                    comp.at[a, 2 + w], got_one.at[a, w], tree_send.at[a, 2 + w], tree_recv.at[a, 2 + w],
                    here.near(0, -step[w]),
                )
            )

    def sum_home(a, out):
        for w in range(2):
            tree[a, 2 + w].wait_recv()
        spread(a, 0, [got_one.at[a, 0], got_one.at[a, 1]], out)

    first_hop(0)
    about = []
    for i in range(1, 5):
        depth, way = STEPS[i]
        about.append(
            start(remote(metas.at[0], metas.at[i], meta_send.at[i - 1], meta_recv.at[i - 1], here.near(0, way * depth)))
        )
    loads[0].wait()
    pick(0, 0)
    second_hop(0)
    for copy in about:
        copy.wait_recv()
    pick(0, 1)
    pick(0, 2)
    loads[1].wait()
    pick(1, 0)
    early = [hop[0, i, 0] for i in (3, 4)]
    for copy in early:
        copy.wait_recv()
    first_hop(1)
    pick(0, 3)
    pick(0, 4)
    second_hop(1)
    pick(1, 1)
    pick(1, 2)
    collect(0)
    send_twin_rows()
    for load in loads[2:]:
        load.wait()
    whole(0)
    forward(0)
    forward(1)
    pick(1, 3)
    pick(1, 4)
    activate()
    forward_out()
    swap_halves(0)
    collect(1)
    send_rows(0)
    hidden_turned = hidden[...].T
    whole(1)
    down_terms(hidden_turned, opposite)
    send_ring()
    backward_hidden()
    send_twin_slopes()
    pass_twin_rows()
    down_terms(hidden_turned, chunk_of[0])
    down_terms(hidden_turned, chunk_of[1])
    send_plain()
    for i in range(1, 5):
        for a in range(2):
            for h in range(2):
                sent(hop[a, i, h])
    sum_two(0)
    ring_step()
    down_terms(hidden_turned, here.y)
    for j in range(16):
        sent(pair[1, j])
    backward_rows()
    swap_halves(1)
    sum_one(0)
    send_rows(1)
    turned = [slopes[p].T for p in range(2)]
    twin[1].wait_recv()
    twin_turned = []
    for p in range(2):
        twin[2 + p].wait_recv()
        twin_turned.append(twin_slopes[p].T)
        wide_terms(p, 1 - home_part, turned[p], twin_turned[p])
        send_mate(p, 0)
    for p in range(2):
        send_mate(p, 1)
    for p in range(2):
        wide_terms(p, home_part, turned[p], twin_turned[p])
    sum_two(1)
    cross_wide(0)
    cross_wide(1)
    sum_home(0, mixed)
    sum_one(1)
    cross_down()
    last_down()
    last_wide(0)
    last_wide(1)
    sum_home(1, input_grad)
    for copy in waiting:
        copy.wait_send()


OUTS = ((TOK, HALF), (TOK, HALF), (512, FF), (512, FF), (FF, 512))


def layer(tok, cot, routes, gates, dropped, placement, w_gate, w_up, w_down):
    vmem = pl.BlockSpec(memory_space=pltpu.VMEM)
    hbm = pl.BlockSpec(memory_space=pl.ANY)
    smem = pl.BlockSpec(memory_space=pltpu.SMEM)
    dma = pltpu.SemaphoreType.DMA
    return pl.pallas_call(
        layer_kernel,
        out_shape=tuple(jax.ShapeDtypeStruct(shape, BF) for shape in OUTS),
        in_specs=[hbm, hbm, vmem, vmem, vmem, smem, hbm, hbm, hbm],
        out_specs=(vmem,) * 5,
        scratch_shapes=[
            pltpu.VMEM((TOK, HALF), BF),
            pltpu.VMEM((TOK, HALF), BF),
            pltpu.VMEM((5, 8, TOK), F32),
            pltpu.VMEM((2, 4, TOK, HALF), BF),
            pltpu.VMEM((2, 11, CAP, HALF), BF),
            pltpu.VMEM((ROWS, FULL), BF),
            pltpu.VMEM((ROWS, FULL), BF),
            pltpu.VMEM((FULL, 2 * FF), BF),
            pltpu.VMEM((FF, FULL), BF),
            pltpu.VMEM((ROWS, 2 * FF), F32),
            pltpu.VMEM((ROWS, FF), BF),
            pltpu.VMEM((2, ROWS, FF), BF),
            pltpu.VMEM((ROWS, FULL), BF),
            pltpu.VMEM((ROWS, HALF), BF),
            pltpu.VMEM((2, ROWS, FF), BF),
            pltpu.VMEM((2 * FF, HALF), BF),
            pltpu.VMEM((FF, FULL), BF),
            pltpu.VMEM((2, ROWS, HALF), BF),
            pltpu.VMEM((2, 5, CAP, HALF), BF),
            pltpu.VMEM((2, 2, 3, CAP, HALF), BF),
            pltpu.VMEM((2, 2, TOK, HALF), BF),
            pltpu.VMEM((2, 2, TOK, HALF), BF),
            pltpu.VMEM((2, 2, FF, 512), BF),
            pltpu.VMEM((2, FF, 512), BF),
            pltpu.VMEM((2, FF, 512), BF),
            pltpu.VMEM((2, 2, FF, 512), BF),
            pltpu.VMEM((FF, 512), BF),
            dma((4,)), dma((4,)),
            dma((2, 4, 2)), dma((2, 4, 2)),
            dma((2, 11)), dma((2, 11)),
            dma((2, 16)), dma((2, 16)),
            dma((2, 2)), dma((2, 2)),
            dma((2, 5)), dma((2, 5)),
            dma((2, 2, 3)), dma((2, 2, 3)),
            dma((2, 4)), dma((2, 4)),
            dma((2,)), dma((2,)),
            dma((2,)), dma((2,)),
            dma((2,)), dma((2,)),
            dma((2, 2)), dma((2, 2)),
            dma((3,)), dma((3,)),
            dma((4,)), dma((4,)),
            dma((5,)),
        ],
        compiler_params=pltpu.CompilerParams(
            collective_id=1, has_side_effects=True, vmem_limit_bytes=63 * MIB
        ),
        name="layer",
    )(tok, cot, routes, gates, dropped, placement, w_gate, w_up, w_down)


def finish_kernel(*refs):
    count = len(OUTS)
    held, load_sem, store_sem = refs[2 * count : 3 * count], refs[3 * count], refs[3 * count + 1]
    loads = [pltpu.make_async_copy(refs[i], held[i], load_sem.at[i]) for i in range(count)]
    stores = [pltpu.make_async_copy(held[i], refs[count + i], store_sem.at[i]) for i in range(count)]
    for load in loads:
        load.start()
    for load, store in zip(loads, stores):
        load.wait()
        store.start()
    for store in stores:
        store.wait()


def finish(*arrays):
    hbm = pl.BlockSpec(memory_space=pl.ANY)
    return pl.pallas_call(
        finish_kernel,
        out_shape=tuple(jax.ShapeDtypeStruct(shape, BF) for shape in OUTS),
        in_specs=[hbm] * len(OUTS),
        out_specs=(hbm,) * len(OUTS),
        scratch_shapes=[pltpu.VMEM(shape, BF) for shape in OUTS]
        + [pltpu.SemaphoreType.DMA((len(OUTS),))] * 2,
        name="finish",
    )(*arrays)


def per_device(tokens, routes, gates, dropped, placement, w_gate, w_up, w_down, cotangent):
    mixed, input_grad, grad_gate, grad_up, grad_down = finish(
        *layer(tokens, cotangent, routes.T, gates.T, dropped.T, placement, w_gate[0], w_up[0], w_down[0])
    )
    return mixed, input_grad, grad_gate[None], grad_up[None], grad_down[None]


def solution(mesh):
    in_specs = (
        P(("dp", "expert"), "tensor"),
        P(("dp", "expert"), None),
        P(("dp", "expert"), None),
        P(("dp", "expert"), None),
        P(),
        P("expert", None, "tensor"),
        P("expert", None, "tensor"),
        P("expert", "tensor", None),
        P(("dp", "expert"), "tensor"),
    )
    out_specs = (
        P(("dp", "expert"), "tensor"),
        P(("dp", "expert"), "tensor"),
        P("expert", "dp", "tensor"),
        P("expert", "dp", "tensor"),
        P("expert", "tensor", "dp"),
    )
    return jax.shard_map(
        per_device, mesh=mesh, in_specs=in_specs, out_specs=out_specs, check_vma=False
    )
```
